256 devices in a mesh: dp: 8 (over z), ctx: 32 (over y, x, core).
Axes of the slice: x: 4, y: 4, z: 8, core: 2. Of those that a mesh axis runs over, the one named last changes fastest.
Arguments:
- query: bfloat16 [8, 8192, 1792], P('dp', 'ctx'), may hold values from -8 to 8
- keys_values: bfloat16 [8, 8192, 512], P('dp', 'ctx'), may hold values from -8 to 8
- beacon_query: bfloat16 [8, 512, 1792], P('dp', 'ctx'), may hold values from -8 to 8
- beacon_hidden: bfloat16 [8, 512, 3584], P('dp', 'ctx'), may hold values from -6 to 6
- beacon_weight: bfloat16 [3584, 512], P('ctx'), may hold values from -0.09375 to 0.09375
- grad_tokens: bfloat16 [8, 8192, 1792], P('dp', 'ctx'), may hold values from -6 to 6
- grad_beacons: bfloat16 [8, 512, 1792], P('dp', 'ctx'), may hold values from -6 to 6
Outputs:
- tokens_out: bfloat16 [8, 8192, 1792], P('dp', 'ctx')
- beacons_out: bfloat16 [8, 512, 1792], P('dp', 'ctx')
- grad_query: bfloat16 [8, 8192, 1792], P('dp', 'ctx')
- grad_keys_values: bfloat16 [8, 8192, 512], P('dp', 'ctx')
- grad_beacon_query: bfloat16 [8, 512, 1792], P('dp', 'ctx')
- grad_beacon_hidden: bfloat16 [8, 512, 3584], P('dp', 'ctx')
- grad_weight: float32 [3584, 512], P('ctx')
The draws below stay inside these ranges and needn't reach their ends.
All inputs are finite; a program needn't handle non-finite values.
Results may differ from the reference program's by a relative error of at most 0.03.
Values may be sent and summed in bfloat16 or wider, within the bound.
No kernel may reach another device: no remote copies, remote signals or barrier semaphores. Data moves between devices by JAX's collectives and lax.ppermute only.
A program may use at most 128 MiB of HBM per device.

```python
import jax
import jax.numpy as jnp
from jax import lax

D = 3584
H = 14
KVH = 2
HD = 128
INTERVAL = 256
BEACONS = 16
GROUP = 7
SEQ = 8192
NBEAC = 512
BATCH = 8
N_CTX = 32


def draw_query(key, part):
    key = jax.random.fold_in(key, 11)
    values = jnp.clip(jax.random.normal(key, (BATCH, SEQ, H * HD), jnp.float32), -6.0, 6.0)
    return values.astype(jnp.bfloat16)


def draw_keys_values(key, part):
    key = jax.random.fold_in(key, 23)
    values = jnp.clip(jax.random.normal(key, (BATCH, SEQ, 2 * KVH * HD), jnp.float32), -6.0, 6.0)
    return values.astype(jnp.bfloat16)


def draw_beacon_query(key, part):
    key = jax.random.fold_in(key, 37)
    values = jnp.clip(jax.random.normal(key, (BATCH, NBEAC, H * HD), jnp.float32), -6.0, 6.0)
    return values.astype(jnp.bfloat16)


def block_levels(key, shape, split, smallest, largest):
    def one(dim, parts):
        steps = jax.random.uniform(jax.random.fold_in(jax.random.fold_in(key, 6), dim), (parts,), jnp.float32, smallest / len(split), largest / len(split))
        return jnp.repeat(jnp.exp(steps), shape[dim] // parts).reshape((-1,) + (1,) * (len(shape) - dim - 1))

    level = one(*split[0])
    for cut in split[1:]:
        level = level * one(*cut)
    return level


def noise(rng, extent, deviation, most, split=(), held_as=jnp.bfloat16):
    loudness = block_levels(rng, extent, split, -0.22, 0.18) if split else 1.0
    drawn = jax.random.normal(rng, extent, jnp.float32) * deviation * loudness
    return jnp.minimum(jnp.maximum(drawn, -most), most).astype(held_as)


def setup_inputs(seed: int = 0) -> dict:
    streams_of = jax.random.split(jax.random.key(seed), 8)
    return {
        "query": draw_query(jax.random.fold_in(streams_of[7], 71), 0),
        "keys_values": draw_keys_values(jax.random.fold_in(streams_of[7], 71), 0),
        "beacon_query": draw_beacon_query(jax.random.fold_in(streams_of[7], 71), 0),
        "beacon_hidden": noise(streams_of[3], (BATCH, NBEAC, D), 1.0, 6.0, ((0, 8), (1, 32))),
        "beacon_weight": noise(streams_of[4], (D, 2 * KVH * HD), D ** -0.5, 0.09375, ((0, 32),)),
        "grad_tokens": noise(streams_of[5], (BATCH, SEQ, H * HD), 1.0, 6.0, ((0, 8), (1, 32))),
        "grad_beacons": noise(streams_of[6], (BATCH, NBEAC, H * HD), 1.0, 6.0, ((0, 8), (1, 32))),
    }


def allowed_keys(span_len, beacon_count, total_beacons, position):
    row_ids = jnp.arange(span_len + beacon_count, dtype=jnp.int32)[:, None]
    col_ids = jnp.arange(total_beacons + span_len, dtype=jnp.int32)[None, :]
    beacon_row = row_ids >= span_len
    own_start = position * beacon_count
    beacon_rank = row_ids - span_len
    prefix_cols = col_ids < own_start
    own_cols = beacon_row & (col_ids >= own_start) & (col_ids - own_start <= beacon_rank) & (col_ids < total_beacons)
    token_cols = (col_ids >= total_beacons) & (beacon_row | (col_ids - total_beacons <= row_ids))
    return prefix_cols | own_cols | token_cols


def interval_pass(tok_query, tok_kv, bea_query, all_kv, cot_tok, cot_bea, position):
    span_len = tok_query.shape[0]
    beacon_count = bea_query.shape[0]
    total_beacons = all_kv.shape[0]
    row_query = jnp.concatenate([tok_query, bea_query], 0)
    row_cot = jnp.concatenate([cot_tok, cot_bea], 0)
    key_rows = jnp.concatenate([all_kv, tok_kv], 0)
    allowed = allowed_keys(span_len, beacon_count, total_beacons, position)
    factor = HD ** -0.5
    width = GROUP * HD
    out_parts, dq_parts, dk_parts, dv_parts = [], [], [], []
    for kv_group in range(KVH):
        q_group = row_query[:, kv_group * width:(kv_group + 1) * width].reshape(-1, GROUP, HD).astype(jnp.float32)
        c_group = row_cot[:, kv_group * width:(kv_group + 1) * width].reshape(-1, GROUP, HD).astype(jnp.float32)
        k_group = key_rows[:, kv_group * HD:(kv_group + 1) * HD].astype(jnp.float32)
        v_group = key_rows[:, (KVH + kv_group) * HD:(KVH + kv_group + 1) * HD].astype(jnp.float32)
        scores = jnp.einsum("rjd,cd->jrc", q_group, k_group) * factor
        scores = jnp.where(allowed[None], scores, -jnp.inf)
        highest = jnp.max(scores, -1, keepdims=True)
        expo_terms = jnp.exp(scores - highest)
        probs = expo_terms / jnp.sum(expo_terms, -1, keepdims=True)
        weights = lax.optimization_barrier(probs.astype(jnp.bfloat16)).astype(jnp.float32)
        out_parts.append(jnp.einsum("jrc,cd->rjd", weights, v_group).reshape(-1, width))
        dv_parts.append(jnp.einsum("jrc,rjd->cd", weights, c_group))
        dweights = jnp.einsum("rjd,cd->jrc", c_group, v_group)
        centre = jnp.sum(probs * dweights, -1, keepdims=True)
        dscores = lax.optimization_barrier((probs * (dweights - centre)).astype(jnp.bfloat16)).astype(jnp.float32)
        dq_parts.append(jnp.einsum("jrc,cd->rjd", dscores, k_group).reshape(-1, width) * factor)
        dk_parts.append(jnp.einsum("jrc,rjd->cd", dscores, q_group) * factor)
    attended = jnp.concatenate(out_parts, -1).astype(jnp.bfloat16)
    query_grad = jnp.concatenate(dq_parts, -1).astype(jnp.bfloat16)
    key_grad = jnp.concatenate(dk_parts + dv_parts, -1)
    return (attended[:span_len], attended[span_len:], query_grad[:span_len], query_grad[span_len:],
            key_grad[total_beacons:].astype(jnp.bfloat16), key_grad[:total_beacons])


def reference(query, keys_values, beacon_query, beacon_hidden, beacon_weight, grad_tokens, grad_beacons):
    kv_width = beacon_weight.shape[1]
    flat_hidden = beacon_hidden.reshape(BATCH * NBEAC, D)
    beacon_kv = jnp.dot(flat_hidden, beacon_weight, preferred_element_type=jnp.float32).astype(jnp.bfloat16)
    beacon_kv = beacon_kv.reshape(BATCH, NBEAC, kv_width)

    def one_sequence(items):
        seq_query, seq_kv, seq_bquery, seq_beacons, seq_gtok, seq_gbea = items

        def one_interval(carried, inner):
            tq_rows, tkv_rows, bq_rows, gt_rows, gb_rows, position = inner
            result = interval_pass(tq_rows, tkv_rows, bq_rows, seq_beacons, gt_rows, gb_rows, position)
            return carried + result[5], result[:5]

        start_sum = jnp.zeros((NBEAC, kv_width), jnp.float32)
        inputs = (seq_query.reshape(N_CTX, INTERVAL, H * HD), seq_kv.reshape(N_CTX, INTERVAL, kv_width),
                  seq_bquery.reshape(N_CTX, BEACONS, H * HD), seq_gtok.reshape(N_CTX, INTERVAL, H * HD),
                  seq_gbea.reshape(N_CTX, BEACONS, H * HD), jnp.arange(N_CTX, dtype=jnp.int32))
        summed, outputs = lax.scan(one_interval, start_sum, inputs)
        return outputs + (summed,)

    results = lax.map(one_sequence, (query, keys_values, beacon_query, beacon_kv, grad_tokens, grad_beacons))
    tokens_out = results[0].reshape(BATCH, SEQ, H * HD)
    beacons_out = results[1].reshape(BATCH, NBEAC, H * HD)
    grad_query = results[2].reshape(BATCH, SEQ, H * HD)
    grad_beacon_query = results[3].reshape(BATCH, NBEAC, H * HD)
    grad_keys_values = results[4].reshape(BATCH, SEQ, kv_width)
    beacon_grad = results[5].astype(jnp.bfloat16).reshape(BATCH * NBEAC, kv_width)
    grad_hidden = jnp.dot(beacon_grad, beacon_weight.T, preferred_element_type=jnp.float32).astype(jnp.bfloat16)
    grad_weight = jnp.dot(flat_hidden.T, beacon_grad, preferred_element_type=jnp.float32)
    return (tokens_out, beacons_out, grad_query, grad_keys_values, grad_beacon_query,
            grad_hidden.reshape(BATCH, NBEAC, D), grad_weight)
```

```python
import jax
import jax.numpy as jnp
from jax import lax
from jax.sharding import PartitionSpec as P

KVH = 2
HD = 128
GROUP = 7


def allowed_keys(span_len, beacon_count, total_beacons, position):
    row_ids = jnp.arange(span_len + beacon_count, dtype=jnp.int32)[:, None]
    col_ids = jnp.arange(total_beacons + span_len, dtype=jnp.int32)[None, :]
    beacon_row = row_ids >= span_len
    own_start = position * beacon_count
    beacon_rank = row_ids - span_len
    prefix_cols = col_ids < own_start
    own_cols = (
        beacon_row
        & (col_ids >= own_start)
        & (col_ids - own_start <= beacon_rank)
        & (col_ids < total_beacons)
    )
    token_cols = (col_ids >= total_beacons) & (beacon_row | (col_ids - total_beacons <= row_ids))
    return prefix_cols | own_cols | token_cols


def interval_pass(tok_query, tok_kv, bea_query, all_kv, cot_tok, cot_bea, position):
    span_len = tok_query.shape[0]
    total_beacons = all_kv.shape[0]
    row_query = jnp.concatenate([tok_query, bea_query], 0)
    row_cot = jnp.concatenate([cot_tok, cot_bea], 0)
    key_rows = jnp.concatenate([all_kv, tok_kv], 0)
    allowed = allowed_keys(span_len, bea_query.shape[0], total_beacons, position)
    factor = HD ** (-0.5)
    width = GROUP * HD
    out_parts, dq_parts, dk_parts, dv_parts = ([], [], [], [])
    for kv_group in range(KVH):
        q_group = row_query[:, kv_group * width : (kv_group + 1) * width].reshape(-1, GROUP, HD)
        c_group = row_cot[:, kv_group * width : (kv_group + 1) * width].reshape(-1, GROUP, HD)
        k_group = key_rows[:, kv_group * HD : (kv_group + 1) * HD]
        v_group = key_rows[:, (KVH + kv_group) * HD : (KVH + kv_group + 1) * HD]
        scores = (
            jnp.einsum("rjd,cd->jrc", q_group, k_group, preferred_element_type=jnp.float32) * factor
        )
        scores = jnp.where(allowed[None], scores, -jnp.inf)
        highest = jnp.max(scores, -1, keepdims=True)
        expo_terms = jnp.exp(scores - highest)
        probs = expo_terms / jnp.sum(expo_terms, -1, keepdims=True)
        weights = probs.astype(jnp.bfloat16)
        out_parts.append(
            jnp.einsum("jrc,cd->rjd", weights, v_group, preferred_element_type=jnp.float32).reshape(
                -1, width
            )
        )
        dv_parts.append(
            jnp.einsum("jrc,rjd->cd", weights, c_group, preferred_element_type=jnp.float32)
        )
        dweights = jnp.einsum("rjd,cd->jrc", c_group, v_group, preferred_element_type=jnp.float32)
        centre = jnp.sum(probs * dweights, -1, keepdims=True)
        dscores = (probs * (dweights - centre)).astype(jnp.bfloat16)
        dq_parts.append(
            jnp.einsum("jrc,cd->rjd", dscores, k_group, preferred_element_type=jnp.float32).reshape(
                -1, width
            )
            * factor
        )
        dk_parts.append(
            jnp.einsum("jrc,rjd->cd", dscores, q_group, preferred_element_type=jnp.float32) * factor
        )
    attended = jnp.concatenate(out_parts, -1).astype(jnp.bfloat16)
    query_grad = jnp.concatenate(dq_parts, -1).astype(jnp.bfloat16)
    key_grad = jnp.concatenate(dk_parts + dv_parts, -1)
    return (
        attended[:span_len],
        attended[span_len:],
        query_grad[:span_len],
        query_grad[span_len:],
        key_grad[total_beacons:].astype(jnp.bfloat16),
        key_grad[:total_beacons],
    )


def exchange(blocks):
    return lax.all_to_all(blocks, "ctx", 0, 0, tiled=True)


def reduce_blocks(blocks):
    return jnp.sum(exchange(blocks).astype(jnp.float32), 0).astype(jnp.bfloat16)


def gather_rows(rows, count):
    return exchange(jnp.broadcast_to(rows[None], (count,) + rows.shape)).reshape(-1, rows.shape[-1])


def sum_dp(part):
    size = lax.axis_size("dp")
    step = 1
    while step < size:
        sent = part.astype(jnp.bfloat16)
        pairs = [(i, i // (2 * step) * 2 * step + 2 * step - 1 - i % (2 * step)) for i in range(size)]
        part = sent.astype(jnp.float32) + lax.ppermute(sent, "dp", pairs).astype(jnp.float32)
        step *= 2
    return part


def shards(
    query, keys_values, beacon_query, beacon_hidden, beacon_weight, grad_tokens, grad_beacons
):
    position = lax.axis_index("ctx")
    count = lax.axis_size("ctx")
    rows = beacon_hidden.shape[1]
    hidden_rows = beacon_hidden[0]
    full_weight = lax.all_gather(beacon_weight, "ctx", axis=0, tiled=True)
    hidden_cols = exchange(hidden_rows.reshape(rows, count, -1).transpose(1, 0, 2))
    hidden_cols = hidden_cols.reshape(rows * count, -1)
    part_kv = jnp.dot(hidden_cols, beacon_weight, preferred_element_type=jnp.float32)
    own_kv = reduce_blocks(part_kv.astype(jnp.bfloat16).reshape(count, rows, -1))
    all_kv = gather_rows(own_kv, count)
    result = interval_pass(
        query[0], keys_values[0], beacon_query[0], all_kv, grad_tokens[0], grad_beacons[0], position
    )
    tokens_out, beacons_out, query_grad, beacon_qgrad, token_kvgrad, contrib = result
    own_grad = reduce_blocks(contrib.astype(jnp.bfloat16).reshape(count, rows, -1))
    all_grad = gather_rows(own_grad, count)
    hidden_grad = lax.dot_general(
        own_grad, full_weight, (((1,), (1,)), ((), ())), preferred_element_type=jnp.float32
    ).astype(jnp.bfloat16)
    weight_part = lax.dot_general(
        hidden_cols, all_grad, (((0,), (0,)), ((), ())), preferred_element_type=jnp.float32
    )
    grad_weight = sum_dp(weight_part)
    return (
        tokens_out[None],
        beacons_out[None],
        query_grad[None],
        token_kvgrad[None],
        beacon_qgrad[None],
        hidden_grad[None],
        grad_weight,
    )


def solution(mesh):
    placed = (
        P("dp", "ctx", None),
        P("dp", "ctx", None),
        P("dp", "ctx", None),
        P("dp", "ctx", None),
        P("ctx", None),
        P("dp", "ctx", None),
        P("dp", "ctx", None),
    )
    return jax.shard_map(
        shards,
        mesh=mesh,
        in_specs=placed,
        out_specs=(
            P("dp", "ctx", None),
            P("dp", "ctx", None),
            P("dp", "ctx", None),
            P("dp", "ctx", None),
            P("dp", "ctx", None),
            P("dp", "ctx", None),
            P("ctx", None),
        ),
        check_vma=False,
    )
```

```python
import jax
import jax.numpy as jnp
from jax import lax
from jax.experimental import pallas as pl
from jax.experimental.pallas import tpu as pltpu
from jax.sharding import PartitionSpec as P

KVH = 2
HD = 128
GROUP = 7
MASKED = -1e30
LOG2E = 1.4426950408889634
FACTOR = HD ** (-0.5)


def dot_nt(left, right):
    return lax.dot_general(
        left, right, (((1,), (1,)), ((), ())), preferred_element_type=jnp.float32
    )


def dot_nn(left, right):
    return jnp.dot(left, right, preferred_element_type=jnp.float32)


def head_rows(tokens_ref, beacons_ref, group, head):
    if head < GROUP:
        start = (group * GROUP + head) * HD
        return tokens_ref[:, start : start + HD]
    parts = []
    for each in range(GROUP):
        start = (group * GROUP + each) * HD
        parts.append(beacons_ref[:, start : start + HD])
    rows = beacons_ref.shape[0]
    parts.append(jnp.zeros((HD - GROUP * rows, HD), beacons_ref.dtype))
    return jnp.concatenate(parts, 0)


def token_bias(span):
    col = lax.broadcasted_iota(jnp.int32, (span, span), 0)
    row = lax.broadcasted_iota(jnp.int32, (span, span), 1)
    return jnp.where(col <= row, 0.0, MASKED).astype(jnp.float32)


def prefix_bias(total, width, start, rank_rows):
    col = lax.broadcasted_iota(jnp.int32, (total, width), 0)
    limit = start
    if rank_rows is not None:
        lane = lax.broadcasted_iota(jnp.int32, (total, width), 1)
        limit = start + 1 + (lane & (rank_rows - 1))
    return jnp.where(col < limit, 0.0, MASKED).astype(jnp.float32)


def token_stats_kernel(q_ref, bq_ref, kv_ref, c_ref, bc_ref, stats_ref, bias_ref):
    span = q_ref.shape[0]
    bias_ref[...] = token_bias(span)
    for group in range(KVH):
        keys = kv_ref[:, group * HD : (group + 1) * HD]
        vals = kv_ref[:, (KVH + group) * HD : (KVH + group + 1) * HD]
        for head in range(GROUP + 1):
            query = head_rows(q_ref, bq_ref, group, head)
            cot = head_rows(c_ref, bc_ref, group, head)
            width = query.shape[0]
            scores = dot_nt(keys, query) * (FACTOR * LOG2E)
            if head < GROUP:
                scores = scores + bias_ref[...]
            top = jnp.max(scores, 0, keepdims=True)
            expo = jnp.exp2(scores - top)
            dweights = dot_nt(vals, cot)
            stats_ref[0, group, head : head + 1, :width] = top
            stats_ref[1, group, head : head + 1, :width] = jnp.sum(expo, 0, keepdims=True)
            stats_ref[2, group, head : head + 1, :width] = jnp.sum(
                expo * dweights, 0, keepdims=True
            )


def beacon_grad_kernel(
    pos_ref, q_ref, bq_ref, kv_ref, c_ref, bc_ref, stats_ref, contrib_ref, rows_ref, bias_ref, bbias_ref
):
    total = kv_ref.shape[0]
    span = q_ref.shape[0]
    count = bq_ref.shape[0]
    start = pos_ref[0] * count
    bias_ref[...] = prefix_bias(total, span, start, None)
    bbias_ref[...] = prefix_bias(total, HD, start, count)
    for group in range(KVH):
        keys = kv_ref[:, group * HD : (group + 1) * HD]
        vals = kv_ref[:, (KVH + group) * HD : (KVH + group + 1) * HD]
        key_grad = jnp.zeros((total, HD), jnp.float32)
        val_grad = jnp.zeros((total, HD), jnp.float32)
        for head in range(GROUP + 1):
            query = head_rows(q_ref, bq_ref, group, head)
            cot = head_rows(c_ref, bc_ref, group, head)
            width = query.shape[0]
            bias = bias_ref if head < GROUP else bbias_ref
            scores = dot_nt(keys, query) * (FACTOR * LOG2E) + bias[...]
            top_tok = stats_ref[0, group, head : head + 1, :width]
            sum_tok = stats_ref[1, group, head : head + 1, :width]
            cen_tok = stats_ref[2, group, head : head + 1, :width]
            top = jnp.maximum(jnp.max(scores, 0, keepdims=True), top_tok)
            shift = jnp.exp2(top_tok - top)
            expo = jnp.exp2(scores - top)
            dweights = dot_nt(vals, cot)
            total_sum = shift * sum_tok + jnp.sum(expo, 0, keepdims=True)
            inverse = 1.0 / total_sum
            centre = inverse * (
                shift * cen_tok + jnp.sum(expo * dweights, 0, keepdims=True)
            )
            probs = expo * inverse
            dscores = (probs * (dweights - centre)).astype(jnp.bfloat16)
            key_grad = key_grad + dot_nn(dscores, query)
            val_grad = val_grad + dot_nn(probs.astype(jnp.bfloat16), cot)
            rows_ref[0, group, head : head + 1, :width] = top + jnp.log(total_sum) * LOG2E
            rows_ref[1, group, head : head + 1, :width] = centre
        contrib_ref[:, group * HD : (group + 1) * HD] = (key_grad * FACTOR).astype(jnp.bfloat16)
        contrib_ref[:, (KVH + group) * HD : (KVH + group + 1) * HD] = val_grad.astype(jnp.bfloat16)


def rest_kernel(
    pos_ref, q_ref, bq_ref, bkv_ref, kv_ref, c_ref, bc_ref, rows_ref,
    out_ref, bout_ref, dq_ref, bdq_ref, dkv_ref, bias_ref, bbias_ref, tbias_ref,
):
    total = bkv_ref.shape[0]
    span = q_ref.shape[0]
    count = bq_ref.shape[0]
    start = pos_ref[0] * count
    bias_ref[...] = prefix_bias(total, span, start, None)
    bbias_ref[...] = prefix_bias(total, HD, start, count)
    tbias_ref[...] = token_bias(span)
    for group in range(KVH):
        key_cols = slice(group * HD, (group + 1) * HD)
        val_cols = slice((KVH + group) * HD, (KVH + group + 1) * HD)
        sides = []
        for ref in (bkv_ref, kv_ref):
            keys = ref[:, key_cols]
            vals = ref[:, val_cols]
            sides.append((keys, vals, keys.T, vals.T))
        key_grad = jnp.zeros((span, HD), jnp.float32)
        val_grad = jnp.zeros((span, HD), jnp.float32)
        for head in range(GROUP + 1):
            query = head_rows(q_ref, bq_ref, group, head)
            cot = head_rows(c_ref, bc_ref, group, head)
            width = query.shape[0]
            lse = rows_ref[0, group, head : head + 1, :width]
            centre = rows_ref[1, group, head : head + 1, :width]
            out = None
            dquery = None
            for side in range(2):
                keys, vals, keys_t, vals_t = sides[side]
                scores = dot_nt(keys, query) * (FACTOR * LOG2E) - lse
                if side == 0:
                    scores = scores + (bias_ref if head < GROUP else bbias_ref)[...]
                elif head < GROUP:
                    scores = scores + tbias_ref[...]
                probs = jnp.exp2(scores)
                dscores = (probs * (dot_nt(vals, cot) - centre)).astype(jnp.bfloat16)
                weights = probs.astype(jnp.bfloat16)
                out_part = dot_nn(vals_t, weights)
                dq_part = dot_nn(keys_t, dscores)
                out = out_part if out is None else out + out_part
                dquery = dq_part if dquery is None else dquery + dq_part
                if side == 1:
                    key_grad = key_grad + dot_nn(dscores, query)
                    val_grad = val_grad + dot_nn(weights, cot)
            out = out.T.astype(jnp.bfloat16)
            dquery = (dquery * FACTOR).T.astype(jnp.bfloat16)
            if head < GROUP:
                at = (group * GROUP + head) * HD
                out_ref[:, at : at + HD] = out
                dq_ref[:, at : at + HD] = dquery
            else:
                for each in range(GROUP):
                    at = (group * GROUP + each) * HD
                    bout_ref[:, at : at + HD] = out[each * count : (each + 1) * count]
                    bdq_ref[:, at : at + HD] = dquery[each * count : (each + 1) * count]
        dkv_ref[:, key_cols] = (key_grad * FACTOR).astype(jnp.bfloat16)
        dkv_ref[:, val_cols] = val_grad.astype(jnp.bfloat16)


VM = pl.BlockSpec(memory_space=pltpu.VMEM)
SM = pl.BlockSpec(memory_space=pltpu.SMEM)


def call(kernel, outs, scratch, specs, args, flops):
    return pl.pallas_call(
        kernel,
        out_shape=outs,
        in_specs=specs,
        out_specs=tuple(VM for _ in outs),
        scratch_shapes=scratch,
        compiler_params=pltpu.CompilerParams(vmem_limit_bytes=40 * 1024 * 1024),
        cost_estimate=pl.CostEstimate(
            flops=flops, bytes_accessed=4 * 1024 * 1024, transcendentals=0
        ),
    )(*args)


def token_stats(query, beacon_query, kv, cot, beacon_cot):
    span = query.shape[0]
    return call(
        token_stats_kernel,
        (jax.ShapeDtypeStruct((3, KVH, GROUP + 1, span), jnp.float32),),
        [pltpu.VMEM((span, span), jnp.float32)],
        [VM] * 5,
        (query, beacon_query, kv, cot, beacon_cot),
        4 * span * span * HD * KVH * (GROUP + 1),
    )[0]


def beacon_grads(pos, query, beacon_query, all_kv, cot, beacon_cot, stats):
    span = query.shape[0]
    total = all_kv.shape[0]
    return call(
        beacon_grad_kernel,
        (
            jax.ShapeDtypeStruct(all_kv.shape, jnp.bfloat16),
            jax.ShapeDtypeStruct((2, KVH, GROUP + 1, span), jnp.float32),
        ),
        [pltpu.VMEM((total, span), jnp.float32), pltpu.VMEM((total, HD), jnp.float32)],
        [SM] + [VM] * 6,
        (pos, query, beacon_query, all_kv, cot, beacon_cot, stats),
        8 * span * total * HD * KVH * (GROUP + 1),
    )


def rest(pos, query, beacon_query, all_kv, kv, cot, beacon_cot, rows):
    span = query.shape[0]
    total = all_kv.shape[0]
    like = lambda x: jax.ShapeDtypeStruct(x.shape, jnp.bfloat16)
    return call(
        rest_kernel,
        (like(query), like(beacon_query), like(query), like(beacon_query), like(kv)),
        [
            pltpu.VMEM((total, span), jnp.float32),
            pltpu.VMEM((total, HD), jnp.float32),
            pltpu.VMEM((span, span), jnp.float32),
        ],
        [SM] + [VM] * 7,
        (pos, query, beacon_query, all_kv, kv, cot, beacon_cot, rows),
        10 * span * (total + span) * HD * KVH * (GROUP + 1),
    )


def exchange(blocks):
    return lax.all_to_all(blocks, "ctx", 0, 0, tiled=True)


def reduce_blocks(blocks):
    return jnp.sum(exchange(blocks).astype(jnp.float32), 0).astype(jnp.bfloat16)


def gather_rows(rows, count):
    return exchange(jnp.broadcast_to(rows[None], (count,) + rows.shape)).reshape(-1, rows.shape[-1])


def sum_dp(part):
    size = lax.axis_size("dp")
    step = 1
    while step < size:
        sent = part.astype(jnp.bfloat16)
        pairs = [(i, i // (2 * step) * 2 * step + 2 * step - 1 - i % (2 * step)) for i in range(size)]
        part = sent.astype(jnp.float32) + lax.ppermute(sent, "dp", pairs).astype(jnp.float32)
        step *= 2
    return part


def shards(
    query, keys_values, beacon_query, beacon_hidden, beacon_weight, grad_tokens, grad_beacons
):
    pos = lax.axis_index("ctx").astype(jnp.int32).reshape(1)
    count = lax.axis_size("ctx")
    rows = beacon_hidden.shape[1]
    hidden_rows = beacon_hidden[0]
    full_weight = lax.all_gather(beacon_weight, "ctx", axis=0, tiled=True)
    stats = token_stats(
        query[0], beacon_query[0], keys_values[0], grad_tokens[0], grad_beacons[0]
    )
    hidden_cols = exchange(hidden_rows.reshape(rows, count, -1).transpose(1, 0, 2))
    hidden_cols = hidden_cols.reshape(rows * count, -1)
    part_kv = jnp.dot(hidden_cols, beacon_weight, preferred_element_type=jnp.float32)
    own_kv = reduce_blocks(part_kv.astype(jnp.bfloat16).reshape(count, rows, -1))
    all_kv = gather_rows(own_kv, count)
    contrib, row_stats = beacon_grads(
        pos, query[0], beacon_query[0], all_kv, grad_tokens[0], grad_beacons[0], stats
    )
    tokens_out, beacons_out, query_grad, beacon_qgrad, token_kvgrad = rest(
        pos, query[0], beacon_query[0], all_kv, keys_values[0], grad_tokens[0], grad_beacons[0], row_stats
    )
    own_grad = reduce_blocks(contrib.reshape(count, rows, -1))
    all_grad = gather_rows(own_grad, count)
    hidden_grad = lax.dot_general(
        own_grad, full_weight, (((1,), (1,)), ((), ())), preferred_element_type=jnp.float32
    ).astype(jnp.bfloat16)
    weight_part = lax.dot_general(
        hidden_cols, all_grad, (((0,), (0,)), ((), ())), preferred_element_type=jnp.float32
    )
    grad_weight = sum_dp(weight_part)
    return (
        tokens_out[None],
        beacons_out[None],
        query_grad[None],
        token_kvgrad[None],
        beacon_qgrad[None],
        hidden_grad[None],
        grad_weight,
    )


def solution(mesh):
    placed = (
        P("dp", "ctx", None),
        P("dp", "ctx", None),
        P("dp", "ctx", None),
        P("dp", "ctx", None),
        P("ctx", None),
        P("dp", "ctx", None),
        P("dp", "ctx", None),
    )
    return jax.shard_map(
        shards,
        mesh=mesh,
        in_specs=placed,
        out_specs=(
            P("dp", "ctx", None),
            P("dp", "ctx", None),
            P("dp", "ctx", None),
            P("dp", "ctx", None),
            P("dp", "ctx", None),
            P("dp", "ctx", None),
            P("ctx", None),
        ),
        check_vma=False,
    )
```

```python
import jax
import jax.numpy as jnp
from jax import lax
from jax.experimental import pallas as pl
from jax.experimental.pallas import tpu as pltpu
from jax.sharding import PartitionSpec as P

KVH = 2
HD = 128
GROUP = 7
MASKED = -1e30
LOG2E = 1.4426950408889634
FACTOR = HD ** (-0.5)


def dot_nt(left, right):
    return lax.dot_general(
        left, right, (((1,), (1,)), ((), ())), preferred_element_type=jnp.float32
    )


def dot_nn(left, right):
    return jnp.dot(left, right, preferred_element_type=jnp.float32)


def head_rows(tokens_ref, beacons_ref, group, head):
    if head < GROUP:
        start = (group * GROUP + head) * HD
        return tokens_ref[:, start : start + HD]
    parts = []
    for each in range(GROUP):
        start = (group * GROUP + each) * HD
        parts.append(beacons_ref[:, start : start + HD])
    rows = beacons_ref.shape[0]
    parts.append(jnp.zeros((HD - GROUP * rows, HD), beacons_ref.dtype))
    return jnp.concatenate(parts, 0)


def token_bias(span):
    col = lax.broadcasted_iota(jnp.int32, (span, span), 0)
    row = lax.broadcasted_iota(jnp.int32, (span, span), 1)
    return jnp.where(col <= row, 0.0, MASKED).astype(jnp.float32)


def prefix_bias(total, width, start, rank_rows):
    col = lax.broadcasted_iota(jnp.int32, (total, width), 0)
    limit = start
    if rank_rows is not None:
        lane = lax.broadcasted_iota(jnp.int32, (total, width), 1)
        limit = start + 1 + (lane & (rank_rows - 1))
    return jnp.where(col < limit, 0.0, MASKED).astype(jnp.float32)


def token_stats_kernel(q_ref, bq_ref, kv_ref, c_ref, bc_ref, stats_ref, bias_ref):
    span = q_ref.shape[0]
    bias_ref[...] = token_bias(span)
    for group in range(KVH):
        keys = kv_ref[:, group * HD : (group + 1) * HD]
        vals = kv_ref[:, (KVH + group) * HD : (KVH + group + 1) * HD]
        for head in range(GROUP + 1):
            query = head_rows(q_ref, bq_ref, group, head)
            cot = head_rows(c_ref, bc_ref, group, head)
            width = query.shape[0]
            scores = dot_nt(keys, query) * (FACTOR * LOG2E)
            if head < GROUP:
                scores = scores + bias_ref[...]
            top = jnp.max(scores, 0, keepdims=True)
            expo = jnp.exp2(scores - top)
            dweights = dot_nt(vals, cot)
            stats_ref[0, group, head : head + 1, :width] = top
            stats_ref[1, group, head : head + 1, :width] = jnp.sum(expo, 0, keepdims=True)
            stats_ref[2, group, head : head + 1, :width] = jnp.sum(
                expo * dweights, 0, keepdims=True
            )


def beacon_grad_kernel(
    pos_ref, q_ref, bq_ref, kv_ref, c_ref, bc_ref, stats_ref, contrib_ref, rows_ref, bias_ref, bbias_ref
):
    total = kv_ref.shape[0]
    span = q_ref.shape[0]
    count = bq_ref.shape[0]
    start = pos_ref[0] * count
    bias_ref[...] = prefix_bias(total, span, start, None)
    bbias_ref[...] = prefix_bias(total, HD, start, count)
    for group in range(KVH):
        keys = kv_ref[:, group * HD : (group + 1) * HD]
        vals = kv_ref[:, (KVH + group) * HD : (KVH + group + 1) * HD]
        key_grad = jnp.zeros((total, HD), jnp.float32)
        val_grad = jnp.zeros((total, HD), jnp.float32)
        for head in range(GROUP + 1):
            query = head_rows(q_ref, bq_ref, group, head)
            cot = head_rows(c_ref, bc_ref, group, head)
            width = query.shape[0]
            bias = bias_ref if head < GROUP else bbias_ref
            scores = dot_nt(keys, query) * (FACTOR * LOG2E) + bias[...]
            top_tok = stats_ref[0, group, head : head + 1, :width]
            sum_tok = stats_ref[1, group, head : head + 1, :width]
            cen_tok = stats_ref[2, group, head : head + 1, :width]
            top = jnp.maximum(jnp.max(scores, 0, keepdims=True), top_tok)
            shift = jnp.exp2(top_tok - top)
            expo = jnp.exp2(scores - top)
            dweights = dot_nt(vals, cot)
            total_sum = shift * sum_tok + jnp.sum(expo, 0, keepdims=True)
            inverse = 1.0 / total_sum
            centre = inverse * (
                shift * cen_tok + jnp.sum(expo * dweights, 0, keepdims=True)
            )
            probs = expo * inverse
            dscores = (probs * (dweights - centre)).astype(jnp.bfloat16)
            key_grad = key_grad + dot_nn(dscores, query)
            val_grad = val_grad + dot_nn(probs.astype(jnp.bfloat16), cot)
            rows_ref[0, group, head : head + 1, :width] = top + jnp.log(total_sum) * LOG2E
            rows_ref[1, group, head : head + 1, :width] = centre
        contrib_ref[:, group * HD : (group + 1) * HD] = (key_grad * FACTOR).astype(jnp.bfloat16)
        contrib_ref[:, (KVH + group) * HD : (KVH + group + 1) * HD] = val_grad.astype(jnp.bfloat16)


def rest_kernel(
    pos_ref, q_ref, bq_ref, bkv_ref, kv_ref, c_ref, bc_ref, rows_ref,
    out_ref, bout_ref, dq_ref, bdq_ref, dkv_ref, bias_ref, bbias_ref, tbias_ref,
):
    total = bkv_ref.shape[0]
    span = q_ref.shape[0]
    count = bq_ref.shape[0]
    start = pos_ref[0] * count
    bias_ref[...] = prefix_bias(total, span, start, None)
    bbias_ref[...] = prefix_bias(total, HD, start, count)
    tbias_ref[...] = token_bias(span)
    for group in range(KVH):
        key_cols = slice(group * HD, (group + 1) * HD)
        val_cols = slice((KVH + group) * HD, (KVH + group + 1) * HD)
        sides = []
        for ref in (bkv_ref, kv_ref):
            keys = ref[:, key_cols]
            vals = ref[:, val_cols]
            sides.append((keys, vals, keys.T, vals.T))
        key_grad = jnp.zeros((span, HD), jnp.float32)
        val_grad = jnp.zeros((span, HD), jnp.float32)
        for head in range(GROUP + 1):
            query = head_rows(q_ref, bq_ref, group, head)
            cot = head_rows(c_ref, bc_ref, group, head)
            width = query.shape[0]
            lse = rows_ref[0, group, head : head + 1, :width]
            centre = rows_ref[1, group, head : head + 1, :width]
            out = None
            dquery = None
            for side in range(2):
                keys, vals, keys_t, vals_t = sides[side]
                scores = dot_nt(keys, query) * (FACTOR * LOG2E) - lse
                if side == 0:
                    scores = scores + (bias_ref if head < GROUP else bbias_ref)[...]
                elif head < GROUP:
                    scores = scores + tbias_ref[...]
                probs = jnp.exp2(scores)
                dscores = (probs * (dot_nt(vals, cot) - centre)).astype(jnp.bfloat16)
                weights = probs.astype(jnp.bfloat16)
                out_part = dot_nn(vals_t, weights)
                dq_part = dot_nn(keys_t, dscores)
                out = out_part if out is None else out + out_part
                dquery = dq_part if dquery is None else dquery + dq_part
                if side == 1:
                    key_grad = key_grad + dot_nn(dscores, query)
                    val_grad = val_grad + dot_nn(weights, cot)
            out = out.T.astype(jnp.bfloat16)
            dquery = (dquery * FACTOR).T.astype(jnp.bfloat16)
            if head < GROUP:
                at = (group * GROUP + head) * HD
                out_ref[:, at : at + HD] = out
                dq_ref[:, at : at + HD] = dquery
            else:
                for each in range(GROUP):
                    at = (group * GROUP + each) * HD
                    bout_ref[:, at : at + HD] = out[each * count : (each + 1) * count]
                    bdq_ref[:, at : at + HD] = dquery[each * count : (each + 1) * count]
        dkv_ref[:, key_cols] = (key_grad * FACTOR).astype(jnp.bfloat16)
        dkv_ref[:, val_cols] = val_grad.astype(jnp.bfloat16)


VM = pl.BlockSpec(memory_space=pltpu.VMEM)
SM = pl.BlockSpec(memory_space=pltpu.SMEM)


def call(kernel, outs, scratch, specs, args, flops):
    return pl.pallas_call(
        kernel,
        out_shape=outs,
        in_specs=specs,
        out_specs=tuple(VM for _ in outs),
        scratch_shapes=scratch,
        compiler_params=pltpu.CompilerParams(vmem_limit_bytes=40 * 1024 * 1024),
        cost_estimate=pl.CostEstimate(
            flops=flops, bytes_accessed=4 * 1024 * 1024, transcendentals=0
        ),
    )(*args)


def token_stats(query, beacon_query, kv, cot, beacon_cot):
    span = query.shape[0]
    return call(
        token_stats_kernel,
        (jax.ShapeDtypeStruct((3, KVH, GROUP + 1, span), jnp.float32),),
        [pltpu.VMEM((span, span), jnp.float32)],
        [VM] * 5,
        (query, beacon_query, kv, cot, beacon_cot),
        4 * span * span * HD * KVH * (GROUP + 1),
    )[0]


def beacon_grads(pos, query, beacon_query, all_kv, cot, beacon_cot, stats):
    span = query.shape[0]
    total = all_kv.shape[0]
    return call(
        beacon_grad_kernel,
        (
            jax.ShapeDtypeStruct(all_kv.shape, jnp.bfloat16),
            jax.ShapeDtypeStruct((2, KVH, GROUP + 1, span), jnp.float32),
        ),
        [pltpu.VMEM((total, span), jnp.float32), pltpu.VMEM((total, HD), jnp.float32)],
        [SM] + [VM] * 6,
        (pos, query, beacon_query, all_kv, cot, beacon_cot, stats),
        8 * span * total * HD * KVH * (GROUP + 1),
    )


def rest(pos, query, beacon_query, all_kv, kv, cot, beacon_cot, rows):
    span = query.shape[0]
    total = all_kv.shape[0]
    like = lambda x: jax.ShapeDtypeStruct(x.shape, jnp.bfloat16)
    return call(
        rest_kernel,
        (like(query), like(beacon_query), like(query), like(beacon_query), like(kv)),
        [
            pltpu.VMEM((total, span), jnp.float32),
            pltpu.VMEM((total, HD), jnp.float32),
            pltpu.VMEM((span, span), jnp.float32),
        ],
        [SM] + [VM] * 7,
        (pos, query, beacon_query, all_kv, kv, cot, beacon_cot, rows),
        10 * span * (total + span) * HD * KVH * (GROUP + 1),
    )


def exchange(blocks):
    return lax.all_to_all(blocks, "ctx", 0, 0, tiled=True)


def reduce_blocks(blocks):
    return jnp.sum(exchange(blocks).astype(jnp.float32), 0).astype(jnp.bfloat16)


def gather_rows(rows, count):
    return exchange(jnp.broadcast_to(rows[None], (count,) + rows.shape)).reshape(-1, rows.shape[-1])


def sum_dp(part):
    size = lax.axis_size("dp")
    step = 1
    while step < size:
        sent = part.astype(jnp.bfloat16)
        pairs = [(i, i // (2 * step) * 2 * step + 2 * step - 1 - i % (2 * step)) for i in range(size)]
        part = sent.astype(jnp.float32) + lax.ppermute(sent, "dp", pairs).astype(jnp.float32)
        step *= 2
    return part


def shards(
    query, keys_values, beacon_query, beacon_hidden, beacon_weight, grad_tokens, grad_beacons
):
    pos = lax.axis_index("ctx").astype(jnp.int32).reshape(1)
    count = lax.axis_size("ctx")
    rows = beacon_hidden.shape[1]
    hidden_rows = beacon_hidden[0]
    full_weight = lax.all_gather(beacon_weight, "ctx", axis=0, tiled=True)
    stats = token_stats(
        query[0], beacon_query[0], keys_values[0], grad_tokens[0], grad_beacons[0]
    )
    hidden_cols = exchange(hidden_rows.reshape(rows, count, -1).transpose(1, 0, 2))
    hidden_cols = hidden_cols.reshape(rows * count, -1)
    part_kv = jnp.dot(hidden_cols, beacon_weight, preferred_element_type=jnp.float32)
    own_kv = reduce_blocks(part_kv.astype(jnp.bfloat16).reshape(count, rows, -1))
    all_kv = gather_rows(own_kv, count)
    contrib, row_stats = beacon_grads(
        pos, query[0], beacon_query[0], all_kv, grad_tokens[0], grad_beacons[0], stats
    )
    others = rest(
        pos, query[0], beacon_query[0], all_kv, keys_values[0], grad_tokens[0], grad_beacons[0], row_stats
    )
    arrived = exchange(contrib.reshape(count, rows, -1))
    arrived, others = lax.optimization_barrier((arrived, others))
    tokens_out, beacons_out, query_grad, beacon_qgrad, token_kvgrad = others
    own_grad = jnp.sum(arrived.astype(jnp.float32), 0).astype(jnp.bfloat16)
    all_grad = gather_rows(own_grad, count)
    hidden_grad = lax.dot_general(
        own_grad, full_weight, (((1,), (1,)), ((), ())), preferred_element_type=jnp.float32
    ).astype(jnp.bfloat16)
    all_grad, hidden_grad = lax.optimization_barrier((all_grad, hidden_grad))
    weight_part = lax.dot_general(
        hidden_cols, all_grad, (((0,), (0,)), ((), ())), preferred_element_type=jnp.float32
    )
    grad_weight = sum_dp(weight_part)
    return (
        tokens_out[None],
        beacons_out[None],
        query_grad[None],
        token_kvgrad[None],
        beacon_qgrad[None],
        hidden_grad[None],
        grad_weight,
    )


def solution(mesh):
    placed = (
        P("dp", "ctx", None),
        P("dp", "ctx", None),
        P("dp", "ctx", None),
        P("dp", "ctx", None),
        P("ctx", None),
        P("dp", "ctx", None),
        P("dp", "ctx", None),
    )
    return jax.shard_map(
        shards,
        mesh=mesh,
        in_specs=placed,
        out_specs=(
            P("dp", "ctx", None),
            P("dp", "ctx", None),
            P("dp", "ctx", None),
            P("dp", "ctx", None),
            P("dp", "ctx", None),
            P("dp", "ctx", None),
            P("ctx", None),
        ),
        check_vma=False,
    )
```

```python
import jax
import jax.numpy as jnp
from jax import lax
from jax.experimental import pallas as pl
from jax.experimental.pallas import tpu as pltpu
from jax.sharding import PartitionSpec as P

KVH = 2
HD = 128
GROUP = 7
MASKED = -1e30
LOG2E = 1.4426950408889634
FACTOR = HD ** (-0.5)


def dot_nt(left, right):
    return lax.dot_general(
        left, right, (((1,), (1,)), ((), ())), preferred_element_type=jnp.float32
    )


def dot_nn(left, right):
    return jnp.dot(left, right, preferred_element_type=jnp.float32)


def head_rows(tokens_ref, beacons_ref, group, head):
    if head < GROUP:
        start = (group * GROUP + head) * HD
        return tokens_ref[:, start : start + HD]
    parts = []
    for each in range(GROUP):
        start = (group * GROUP + each) * HD
        parts.append(beacons_ref[:, start : start + HD])
    rows = beacons_ref.shape[0]
    parts.append(jnp.zeros((HD - GROUP * rows, HD), beacons_ref.dtype))
    return jnp.concatenate(parts, 0)


def token_bias(span):
    col = lax.broadcasted_iota(jnp.int32, (span, span), 0)
    row = lax.broadcasted_iota(jnp.int32, (span, span), 1)
    return jnp.where(col <= row, 0.0, MASKED).astype(jnp.float32)


def prefix_bias(total, width, start, rank_rows):
    col = lax.broadcasted_iota(jnp.int32, (total, width), 0)
    limit = start
    if rank_rows is not None:
        lane = lax.broadcasted_iota(jnp.int32, (total, width), 1)
        limit = start + 1 + (lane & (rank_rows - 1))
    return jnp.where(col < limit, 0.0, MASKED).astype(jnp.float32)


def token_stats_kernel(q_ref, bq_ref, kv_ref, c_ref, bc_ref, stats_ref, bias_ref):
    span = q_ref.shape[0]
    bias_ref[...] = token_bias(span)
    for group in range(KVH):
        keys = kv_ref[:, group * HD : (group + 1) * HD]
        vals = kv_ref[:, (KVH + group) * HD : (KVH + group + 1) * HD]
        for head in range(GROUP + 1):
            query = head_rows(q_ref, bq_ref, group, head)
            cot = head_rows(c_ref, bc_ref, group, head)
            width = query.shape[0]
            scores = dot_nt(keys, query) * (FACTOR * LOG2E)
            if head < GROUP:
                scores = scores + bias_ref[...]
            top = jnp.max(scores, 0, keepdims=True)
            expo = jnp.exp2(scores - top)
            dweights = dot_nt(vals, cot)
            stats_ref[0, group, head : head + 1, :width] = top
            stats_ref[1, group, head : head + 1, :width] = jnp.sum(expo, 0, keepdims=True)
            stats_ref[2, group, head : head + 1, :width] = jnp.sum(
                expo * dweights, 0, keepdims=True
            )


def beacon_grad_kernel(
    pos_ref, q_ref, bq_ref, kv_ref, c_ref, bc_ref, stats_ref, contrib_ref, rows_ref, bias_ref, bbias_ref
):
    total = kv_ref.shape[0]
    span = q_ref.shape[0]
    count = bq_ref.shape[0]
    start = pos_ref[0] * count
    bias_ref[...] = prefix_bias(total, span, start, None)
    bbias_ref[...] = prefix_bias(total, HD, start, count)
    for group in range(KVH):
        keys = kv_ref[:, group * HD : (group + 1) * HD]
        vals = kv_ref[:, (KVH + group) * HD : (KVH + group + 1) * HD]
        key_grad = jnp.zeros((total, HD), jnp.float32)
        val_grad = jnp.zeros((total, HD), jnp.float32)
        for head in range(GROUP + 1):
            query = head_rows(q_ref, bq_ref, group, head)
            cot = head_rows(c_ref, bc_ref, group, head)
            width = query.shape[0]
            bias = bias_ref if head < GROUP else bbias_ref
            scores = dot_nt(keys, query) * (FACTOR * LOG2E) + bias[...]
            top_tok = stats_ref[0, group, head : head + 1, :width]
            sum_tok = stats_ref[1, group, head : head + 1, :width]
            cen_tok = stats_ref[2, group, head : head + 1, :width]
            top = jnp.maximum(jnp.max(scores, 0, keepdims=True), top_tok)
            shift = jnp.exp2(top_tok - top)
            expo = jnp.exp2(scores - top)
            dweights = dot_nt(vals, cot)
            total_sum = shift * sum_tok + jnp.sum(expo, 0, keepdims=True)
            inverse = 1.0 / total_sum
            centre = inverse * (
                shift * cen_tok + jnp.sum(expo * dweights, 0, keepdims=True)
            )
            probs = expo * inverse
            dscores = (probs * (dweights - centre)).astype(jnp.bfloat16)
            key_grad = key_grad + dot_nn(dscores, query)
            val_grad = val_grad + dot_nn(probs.astype(jnp.bfloat16), cot)
            rows_ref[0, group, head : head + 1, :width] = top + jnp.log(total_sum) * LOG2E
            rows_ref[1, group, head : head + 1, :width] = centre
        contrib_ref[:, group * HD : (group + 1) * HD] = (key_grad * FACTOR).astype(jnp.bfloat16)
        contrib_ref[:, (KVH + group) * HD : (KVH + group + 1) * HD] = val_grad.astype(jnp.bfloat16)


def rest_kernel(
    pos_ref, q_ref, bq_ref, bkv_ref, kv_ref, c_ref, bc_ref, rows_ref,
    out_ref, bout_ref, dq_ref, bdq_ref, dkv_ref, bias_ref, bbias_ref, tbias_ref,
):
    total = bkv_ref.shape[0]
    span = q_ref.shape[0]
    count = bq_ref.shape[0]
    start = pos_ref[0] * count
    bias_ref[...] = prefix_bias(total, span, start, None)
    bbias_ref[...] = prefix_bias(total, HD, start, count)
    tbias_ref[...] = token_bias(span)
    for group in range(KVH):
        key_cols = slice(group * HD, (group + 1) * HD)
        val_cols = slice((KVH + group) * HD, (KVH + group + 1) * HD)
        sides = []
        for ref in (bkv_ref, kv_ref):
            keys = ref[:, key_cols]
            vals = ref[:, val_cols]
            sides.append((keys, vals, keys.T, vals.T))
        key_grad = jnp.zeros((span, HD), jnp.float32)
        val_grad = jnp.zeros((span, HD), jnp.float32)
        for head in range(GROUP + 1):
            query = head_rows(q_ref, bq_ref, group, head)
            cot = head_rows(c_ref, bc_ref, group, head)
            width = query.shape[0]
            lse = rows_ref[0, group, head : head + 1, :width]
            centre = rows_ref[1, group, head : head + 1, :width]
            out = None
            dquery = None
            for side in range(2):
                keys, vals, keys_t, vals_t = sides[side]
                scores = dot_nt(keys, query) * (FACTOR * LOG2E) - lse
                if side == 0:
                    scores = scores + (bias_ref if head < GROUP else bbias_ref)[...]
                elif head < GROUP:
                    scores = scores + tbias_ref[...]
                probs = jnp.exp2(scores)
                dscores = (probs * (dot_nt(vals, cot) - centre)).astype(jnp.bfloat16)
                weights = probs.astype(jnp.bfloat16)
                out_part = dot_nn(vals_t, weights)
                dq_part = dot_nn(keys_t, dscores)
                out = out_part if out is None else out + out_part
                dquery = dq_part if dquery is None else dquery + dq_part
                if side == 1:
                    key_grad = key_grad + dot_nn(dscores, query)
                    val_grad = val_grad + dot_nn(weights, cot)
            out = out.T.astype(jnp.bfloat16)
            dquery = (dquery * FACTOR).T.astype(jnp.bfloat16)
            if head < GROUP:
                at = (group * GROUP + head) * HD
                out_ref[:, at : at + HD] = out
                dq_ref[:, at : at + HD] = dquery
            else:
                for each in range(GROUP):
                    at = (group * GROUP + each) * HD
                    bout_ref[:, at : at + HD] = out[each * count : (each + 1) * count]
                    bdq_ref[:, at : at + HD] = dquery[each * count : (each + 1) * count]
        dkv_ref[:, key_cols] = (key_grad * FACTOR).astype(jnp.bfloat16)
        dkv_ref[:, val_cols] = val_grad.astype(jnp.bfloat16)


VM = pl.BlockSpec(memory_space=pltpu.VMEM)
SM = pl.BlockSpec(memory_space=pltpu.SMEM)


def call(kernel, outs, scratch, specs, args, flops):
    return pl.pallas_call(
        kernel,
        out_shape=outs,
        in_specs=specs,
        out_specs=tuple(VM for _ in outs),
        scratch_shapes=scratch,
        compiler_params=pltpu.CompilerParams(vmem_limit_bytes=40 * 1024 * 1024),
        cost_estimate=pl.CostEstimate(
            flops=flops, bytes_accessed=4 * 1024 * 1024, transcendentals=0
        ),
    )(*args)


def token_stats(query, beacon_query, kv, cot, beacon_cot):
    span = query.shape[0]
    return call(
        token_stats_kernel,
        (jax.ShapeDtypeStruct((3, KVH, GROUP + 1, span), jnp.float32),),
        [pltpu.VMEM((span, span), jnp.float32)],
        [VM] * 5,
        (query, beacon_query, kv, cot, beacon_cot),
        4 * span * span * HD * KVH * (GROUP + 1),
    )[0]


def beacon_grads(pos, query, beacon_query, all_kv, cot, beacon_cot, stats):
    span = query.shape[0]
    total = all_kv.shape[0]
    return call(
        beacon_grad_kernel,
        (
            jax.ShapeDtypeStruct(all_kv.shape, jnp.bfloat16),
            jax.ShapeDtypeStruct((2, KVH, GROUP + 1, span), jnp.float32),
        ),
        [pltpu.VMEM((total, span), jnp.float32), pltpu.VMEM((total, HD), jnp.float32)],
        [SM] + [VM] * 6,
        (pos, query, beacon_query, all_kv, cot, beacon_cot, stats),
        8 * span * total * HD * KVH * (GROUP + 1),
    )


def rest(pos, query, beacon_query, all_kv, kv, cot, beacon_cot, rows):
    span = query.shape[0]
    total = all_kv.shape[0]
    like = lambda x: jax.ShapeDtypeStruct(x.shape, jnp.bfloat16)
    return call(
        rest_kernel,
        (like(query), like(beacon_query), like(query), like(beacon_query), like(kv)),
        [
            pltpu.VMEM((total, span), jnp.float32),
            pltpu.VMEM((total, HD), jnp.float32),
            pltpu.VMEM((span, span), jnp.float32),
        ],
        [SM] + [VM] * 7,
        (pos, query, beacon_query, all_kv, kv, cot, beacon_cot, rows),
        10 * span * (total + span) * HD * KVH * (GROUP + 1),
    )


def exchange(blocks):
    return lax.all_to_all(blocks, "ctx", 0, 0, tiled=True)


def reduce_blocks(blocks):
    return jnp.sum(exchange(blocks).astype(jnp.float32), 0).astype(jnp.bfloat16)


def gather_rows(rows, count):
    return exchange(jnp.broadcast_to(rows[None], (count,) + rows.shape)).reshape(-1, rows.shape[-1])


def sum_dp(part):
    size = lax.axis_size("dp")
    step = 1
    while step < size:
        sent = part.astype(jnp.bfloat16)
        pairs = [(i, i // (2 * step) * 2 * step + 2 * step - 1 - i % (2 * step)) for i in range(size)]
        part = sent.astype(jnp.float32) + lax.ppermute(sent, "dp", pairs).astype(jnp.float32)
        step *= 2
    return part


def shards(
    query, keys_values, beacon_query, beacon_hidden, beacon_weight, grad_tokens, grad_beacons
):
    pos = lax.axis_index("ctx").astype(jnp.int32).reshape(1)
    count = lax.axis_size("ctx")
    rows = beacon_hidden.shape[1]
    hidden_rows = beacon_hidden[0]
    stats = token_stats(
        query[0], beacon_query[0], keys_values[0], grad_tokens[0], grad_beacons[0]
    )
    hidden_cols = exchange(hidden_rows.reshape(rows, count, -1).transpose(1, 0, 2))
    hidden_cols = hidden_cols.reshape(rows * count, -1)
    part_kv = jnp.dot(hidden_cols, beacon_weight, preferred_element_type=jnp.float32)
    own_kv = reduce_blocks(part_kv.astype(jnp.bfloat16).reshape(count, rows, -1))
    all_kv = gather_rows(own_kv, count)
    contrib, row_stats = beacon_grads(
        pos, query[0], beacon_query[0], all_kv, grad_tokens[0], grad_beacons[0], stats
    )
    others = rest(
        pos, query[0], beacon_query[0], all_kv, keys_values[0], grad_tokens[0], grad_beacons[0], row_stats
    )
    arrived = exchange(contrib.reshape(count, rows, -1))
    arrived, others = lax.optimization_barrier((arrived, others))
    tokens_out, beacons_out, query_grad, beacon_qgrad, token_kvgrad = others
    own_grad = jnp.sum(arrived.astype(jnp.float32), 0).astype(jnp.bfloat16)
    all_grad = gather_rows(own_grad, count)
    weight_part = lax.dot_general(
        hidden_cols, all_grad, (((0,), (0,)), ((), ())), preferred_element_type=jnp.float32
    )
    grad_weight = sum_dp(weight_part)
    hidden_part = lax.dot_general(
        all_grad, beacon_weight, (((1,), (1,)), ((), ())), preferred_element_type=jnp.float32
    ).astype(jnp.bfloat16)
    hidden_grad = exchange(hidden_part.reshape(count, rows, -1)).transpose(1, 0, 2).reshape(rows, -1)
    return (
        tokens_out[None],
        beacons_out[None],
        query_grad[None],
        token_kvgrad[None],
        beacon_qgrad[None],
        hidden_grad[None],
        grad_weight,
    )


def solution(mesh):
    placed = (
        P("dp", "ctx", None),
        P("dp", "ctx", None),
        P("dp", "ctx", None),
        P("dp", "ctx", None),
        P("ctx", None),
        P("dp", "ctx", None),
        P("dp", "ctx", None),
    )
    return jax.shard_map(
        shards,
        mesh=mesh,
        in_specs=placed,
        out_specs=(
            P("dp", "ctx", None),
            P("dp", "ctx", None),
            P("dp", "ctx", None),
            P("dp", "ctx", None),
            P("dp", "ctx", None),
            P("dp", "ctx", None),
            P("ctx", None),
        ),
        check_vma=False,
    )
```

```python
import jax
import jax.numpy as jnp
from jax import lax
from jax.experimental import pallas as pl
from jax.experimental.pallas import tpu as pltpu
from jax.sharding import PartitionSpec as P

KVH = 2
HD = 128
GROUP = 7
MASKED = -1e30
LOG2E = 1.4426950408889634
FACTOR = HD ** (-0.5)


def dot_nt(left, right):
    return lax.dot_general(
        left, right, (((1,), (1,)), ((), ())), preferred_element_type=jnp.float32
    )


def dot_nn(left, right):
    return jnp.dot(left, right, preferred_element_type=jnp.float32)


def head_rows(tokens_ref, beacons_ref, group, head):
    if head < GROUP:
        start = (group * GROUP + head) * HD
        return tokens_ref[:, start : start + HD]
    parts = []
    for each in range(GROUP):
        start = (group * GROUP + each) * HD
        parts.append(beacons_ref[:, start : start + HD])
    rows = beacons_ref.shape[0]
    parts.append(jnp.zeros((HD - GROUP * rows, HD), beacons_ref.dtype))
    return jnp.concatenate(parts, 0)


def token_bias(span):
    col = lax.broadcasted_iota(jnp.int32, (span, span), 0)
    row = lax.broadcasted_iota(jnp.int32, (span, span), 1)
    return jnp.where(col <= row, 0.0, MASKED).astype(jnp.float32)


def prefix_bias(total, width, start, rank_rows):
    col = lax.broadcasted_iota(jnp.int32, (total, width), 0)
    limit = start
    if rank_rows is not None:
        lane = lax.broadcasted_iota(jnp.int32, (total, width), 1)
        limit = start + 1 + (lane & (rank_rows - 1))
    return jnp.where(col < limit, 0.0, MASKED).astype(jnp.float32)


def token_stats_kernel(q_ref, bq_ref, kv_ref, c_ref, bc_ref, stats_ref, bias_ref):
    span = q_ref.shape[0]
    bias_ref[...] = token_bias(span)
    for group in range(KVH):
        keys = kv_ref[:, group * HD : (group + 1) * HD]
        vals = kv_ref[:, (KVH + group) * HD : (KVH + group + 1) * HD]
        for head in range(GROUP + 1):
            query = head_rows(q_ref, bq_ref, group, head)
            cot = head_rows(c_ref, bc_ref, group, head)
            width = query.shape[0]
            scores = dot_nt(keys, query) * (FACTOR * LOG2E)
            if head < GROUP:
                scores = scores + bias_ref[...]
            top = jnp.max(scores, 0, keepdims=True)
            expo = jnp.exp2(scores - top)
            dweights = dot_nt(vals, cot)
            stats_ref[0, group, head : head + 1, :width] = top
            stats_ref[1, group, head : head + 1, :width] = jnp.sum(expo, 0, keepdims=True)
            stats_ref[2, group, head : head + 1, :width] = jnp.sum(
                expo * dweights, 0, keepdims=True
            )


def beacon_grad_kernel(
    pos_ref, q_ref, bq_ref, kv_ref, c_ref, bc_ref, stats_ref, contrib_ref, rows_ref, bias_ref, bbias_ref
):
    total = kv_ref.shape[0]
    span = q_ref.shape[0]
    count = bq_ref.shape[0]
    start = pos_ref[0] * count
    bias_ref[...] = prefix_bias(total, span, start, None)
    bbias_ref[...] = prefix_bias(total, HD, start, count)
    for group in range(KVH):
        keys = kv_ref[:, group * HD : (group + 1) * HD]
        vals = kv_ref[:, (KVH + group) * HD : (KVH + group + 1) * HD]
        key_grad = jnp.zeros((total, HD), jnp.float32)
        val_grad = jnp.zeros((total, HD), jnp.float32)
        for head in range(GROUP + 1):
            query = head_rows(q_ref, bq_ref, group, head)
            cot = head_rows(c_ref, bc_ref, group, head)
            width = query.shape[0]
            bias = bias_ref if head < GROUP else bbias_ref
            scores = dot_nt(keys, query) * (FACTOR * LOG2E) + bias[...]
            top_tok = stats_ref[0, group, head : head + 1, :width]
            sum_tok = stats_ref[1, group, head : head + 1, :width]
            cen_tok = stats_ref[2, group, head : head + 1, :width]
            top = jnp.maximum(jnp.max(scores, 0, keepdims=True), top_tok)
            shift = jnp.exp2(top_tok - top)
            expo = jnp.exp2(scores - top)
            dweights = dot_nt(vals, cot)
            total_sum = shift * sum_tok + jnp.sum(expo, 0, keepdims=True)
            inverse = 1.0 / total_sum
            centre = inverse * (
                shift * cen_tok + jnp.sum(expo * dweights, 0, keepdims=True)
            )
            probs = expo * inverse
            dscores = (probs * (dweights - centre)).astype(jnp.bfloat16)
            key_grad = key_grad + dot_nn(dscores, query)
            val_grad = val_grad + dot_nn(probs.astype(jnp.bfloat16), cot)
            rows_ref[0, group, head : head + 1, :width] = top + jnp.log(total_sum) * LOG2E
            rows_ref[1, group, head : head + 1, :width] = centre
        contrib_ref[:, group * HD : (group + 1) * HD] = (key_grad * FACTOR).astype(jnp.bfloat16)
        contrib_ref[:, (KVH + group) * HD : (KVH + group + 1) * HD] = val_grad.astype(jnp.bfloat16)


def rest_kernel(
    pos_ref, q_ref, bq_ref, bkv_ref, kv_ref, c_ref, bc_ref, rows_ref,
    out_ref, bout_ref, dq_ref, bdq_ref, dkv_ref, bias_ref, bbias_ref, tbias_ref,
):
    total = bkv_ref.shape[0]
    span = q_ref.shape[0]
    count = bq_ref.shape[0]
    start = pos_ref[0] * count
    bias_ref[...] = prefix_bias(total, span, start, None)
    bbias_ref[...] = prefix_bias(total, HD, start, count)
    tbias_ref[...] = token_bias(span)
    for group in range(KVH):
        key_cols = slice(group * HD, (group + 1) * HD)
        val_cols = slice((KVH + group) * HD, (KVH + group + 1) * HD)
        sides = []
        for ref in (bkv_ref, kv_ref):
            keys = ref[:, key_cols]
            vals = ref[:, val_cols]
            sides.append((keys, vals, keys.T, vals.T))
        key_grad = jnp.zeros((span, HD), jnp.float32)
        val_grad = jnp.zeros((span, HD), jnp.float32)
        for head in range(GROUP + 1):
            query = head_rows(q_ref, bq_ref, group, head)
            cot = head_rows(c_ref, bc_ref, group, head)
            width = query.shape[0]
            lse = rows_ref[0, group, head : head + 1, :width]
            centre = rows_ref[1, group, head : head + 1, :width]
            out = None
            dquery = None
            for side in range(2):
                keys, vals, keys_t, vals_t = sides[side]
                scores = dot_nt(keys, query) * (FACTOR * LOG2E) - lse
                if side == 0:
                    scores = scores + (bias_ref if head < GROUP else bbias_ref)[...]
                elif head < GROUP:
                    scores = scores + tbias_ref[...]
                probs = jnp.exp2(scores)
                dscores = (probs * (dot_nt(vals, cot) - centre)).astype(jnp.bfloat16)
                weights = probs.astype(jnp.bfloat16)
                out_part = dot_nn(vals_t, weights)
                dq_part = dot_nn(keys_t, dscores)
                out = out_part if out is None else out + out_part
                dquery = dq_part if dquery is None else dquery + dq_part
                if side == 1:
                    key_grad = key_grad + dot_nn(dscores, query)
                    val_grad = val_grad + dot_nn(weights, cot)
            out = out.T.astype(jnp.bfloat16)
            dquery = (dquery * FACTOR).T.astype(jnp.bfloat16)
            if head < GROUP:
                at = (group * GROUP + head) * HD
                out_ref[:, at : at + HD] = out
                dq_ref[:, at : at + HD] = dquery
            else:
                for each in range(GROUP):
                    at = (group * GROUP + each) * HD
                    bout_ref[:, at : at + HD] = out[each * count : (each + 1) * count]
                    bdq_ref[:, at : at + HD] = dquery[each * count : (each + 1) * count]
        dkv_ref[:, key_cols] = (key_grad * FACTOR).astype(jnp.bfloat16)
        dkv_ref[:, val_cols] = val_grad.astype(jnp.bfloat16)


VM = pl.BlockSpec(memory_space=pltpu.VMEM)
SM = pl.BlockSpec(memory_space=pltpu.SMEM)


def call(kernel, outs, scratch, specs, args, flops):
    return pl.pallas_call(
        kernel,
        out_shape=outs,
        in_specs=specs,
        out_specs=tuple(VM for _ in outs),
        scratch_shapes=scratch,
        compiler_params=pltpu.CompilerParams(vmem_limit_bytes=40 * 1024 * 1024),
        cost_estimate=pl.CostEstimate(
            flops=flops, bytes_accessed=4 * 1024 * 1024, transcendentals=0
        ),
    )(*args)


def token_stats(query, beacon_query, kv, cot, beacon_cot):
    span = query.shape[0]
    return call(
        token_stats_kernel,
        (jax.ShapeDtypeStruct((3, KVH, GROUP + 1, span), jnp.float32),),
        [pltpu.VMEM((span, span), jnp.float32)],
        [VM] * 5,
        (query, beacon_query, kv, cot, beacon_cot),
        4 * span * span * HD * KVH * (GROUP + 1),
    )[0]


def beacon_grads(pos, query, beacon_query, all_kv, cot, beacon_cot, stats):
    span = query.shape[0]
    total = all_kv.shape[0]
    return call(
        beacon_grad_kernel,
        (
            jax.ShapeDtypeStruct(all_kv.shape, jnp.bfloat16),
            jax.ShapeDtypeStruct((2, KVH, GROUP + 1, span), jnp.float32),
        ),
        [pltpu.VMEM((total, span), jnp.float32), pltpu.VMEM((total, HD), jnp.float32)],
        [SM] + [VM] * 6,
        (pos, query, beacon_query, all_kv, cot, beacon_cot, stats),
        8 * span * total * HD * KVH * (GROUP + 1),
    )


def rest(pos, query, beacon_query, all_kv, kv, cot, beacon_cot, rows):
    span = query.shape[0]
    total = all_kv.shape[0]
    like = lambda x: jax.ShapeDtypeStruct(x.shape, jnp.bfloat16)
    return call(
        rest_kernel,
        (like(query), like(beacon_query), like(query), like(beacon_query), like(kv)),
        [
            pltpu.VMEM((total, span), jnp.float32),
            pltpu.VMEM((total, HD), jnp.float32),
            pltpu.VMEM((span, span), jnp.float32),
        ],
        [SM] + [VM] * 7,
        (pos, query, beacon_query, all_kv, kv, cot, beacon_cot, rows),
        10 * span * (total + span) * HD * KVH * (GROUP + 1),
    )


def exchange(blocks):
    return lax.all_to_all(blocks, "ctx", 0, 0, tiled=True)


def reduce_blocks(blocks):
    return jnp.sum(exchange(blocks).astype(jnp.float32), 0).astype(jnp.bfloat16)


def gather_rows(rows, count):
    return exchange(jnp.broadcast_to(rows[None], (count,) + rows.shape)).reshape(-1, rows.shape[-1])


def swap_dp(sent, mask):
    pairs = [(i, i ^ mask) for i in range(lax.axis_size("dp"))]
    return lax.ppermute(sent, "dp", pairs).astype(jnp.float32)


def sum_dp(part, beside):
    sent = part.astype(jnp.bfloat16)
    near, far, wide = [swap_dp(sent, mask) for mask in (2, 4, 6)]
    near, far, wide, beside = lax.optimization_barrier((near, far, wide, beside))
    part = (sent.astype(jnp.float32) + near) + (far + wide)
    sent = part.astype(jnp.bfloat16)
    return sent.astype(jnp.float32) + swap_dp(sent, 1), beside


def shards(
    query, keys_values, beacon_query, beacon_hidden, beacon_weight, grad_tokens, grad_beacons
):
    pos = lax.axis_index("ctx").astype(jnp.int32).reshape(1)
    count = lax.axis_size("ctx")
    rows = beacon_hidden.shape[1]
    hidden_rows = beacon_hidden[0]
    stats = token_stats(
        query[0], beacon_query[0], keys_values[0], grad_tokens[0], grad_beacons[0]
    )
    hidden_cols = exchange(hidden_rows.reshape(rows, count, -1).transpose(1, 0, 2))
    hidden_cols = hidden_cols.reshape(rows * count, -1)
    part_kv = jnp.dot(hidden_cols, beacon_weight, preferred_element_type=jnp.float32)
    own_kv = reduce_blocks(part_kv.astype(jnp.bfloat16).reshape(count, rows, -1))
    all_kv = gather_rows(own_kv, count)
    contrib, row_stats = beacon_grads(
        pos, query[0], beacon_query[0], all_kv, grad_tokens[0], grad_beacons[0], stats
    )
    others = rest(
        pos, query[0], beacon_query[0], all_kv, keys_values[0], grad_tokens[0], grad_beacons[0], row_stats
    )
    arrived = exchange(contrib.reshape(count, rows, -1))
    arrived, others = lax.optimization_barrier((arrived, others))
    tokens_out, beacons_out, query_grad, beacon_qgrad, token_kvgrad = others
    own_grad = jnp.sum(arrived.astype(jnp.float32), 0).astype(jnp.bfloat16)
    all_grad = gather_rows(own_grad, count)
    weight_part = lax.dot_general(
        hidden_cols, all_grad, (((0,), (0,)), ((), ())), preferred_element_type=jnp.float32
    )
    hidden_part = lax.dot_general(
        all_grad, beacon_weight, (((1,), (1,)), ((), ())), preferred_element_type=jnp.float32
    ).astype(jnp.bfloat16)
    hidden_blocks = exchange(hidden_part.reshape(count, rows, -1))
    grad_weight, hidden_blocks = sum_dp(weight_part, hidden_blocks)
    hidden_grad = hidden_blocks.transpose(1, 0, 2).reshape(rows, -1)
    return (
        tokens_out[None],
        beacons_out[None],
        query_grad[None],
        token_kvgrad[None],
        beacon_qgrad[None],
        hidden_grad[None],
        grad_weight,
    )


def solution(mesh):
    placed = (
        P("dp", "ctx", None),
        P("dp", "ctx", None),
        P("dp", "ctx", None),
        P("dp", "ctx", None),
        P("ctx", None),
        P("dp", "ctx", None),
        P("dp", "ctx", None),
    )
    return jax.shard_map(
        shards,
        mesh=mesh,
        in_specs=placed,
        out_specs=(
            P("dp", "ctx", None),
            P("dp", "ctx", None),
            P("dp", "ctx", None),
            P("dp", "ctx", None),
            P("dp", "ctx", None),
            P("dp", "ctx", None),
            P("ctx", None),
        ),
        check_vma=False,
    )
```

```python
import jax
import jax.numpy as jnp
from jax import lax
from jax.experimental import pallas as pl
from jax.experimental.pallas import tpu as pltpu
from jax.sharding import PartitionSpec as P

KVH = 2
HD = 128
GROUP = 7
MASKED = -1e30
LOG2E = 1.4426950408889634
FACTOR = HD ** (-0.5)


def dot_nt(left, right):
    return lax.dot_general(
        left, right, (((1,), (1,)), ((), ())), preferred_element_type=jnp.float32
    )


def dot_nn(left, right):
    return jnp.dot(left, right, preferred_element_type=jnp.float32)


def head_rows(tokens_ref, beacons_ref, group, head):
    if head < GROUP:
        start = (group * GROUP + head) * HD
        return tokens_ref[:, start : start + HD]
    parts = []
    for each in range(GROUP):
        start = (group * GROUP + each) * HD
        parts.append(beacons_ref[:, start : start + HD])
    rows = beacons_ref.shape[0]
    parts.append(jnp.zeros((HD - GROUP * rows, HD), beacons_ref.dtype))
    return jnp.concatenate(parts, 0)


def token_bias(span):
    col = lax.broadcasted_iota(jnp.int32, (span, span), 0)
    row = lax.broadcasted_iota(jnp.int32, (span, span), 1)
    return jnp.where(col <= row, 0.0, MASKED).astype(jnp.float32)


def prefix_bias(total, width, start, rank_rows):
    col = lax.broadcasted_iota(jnp.int32, (total, width), 0)
    limit = start
    if rank_rows is not None:
        lane = lax.broadcasted_iota(jnp.int32, (total, width), 1)
        limit = start + 1 + (lane & (rank_rows - 1))
    return jnp.where(col < limit, 0.0, MASKED).astype(jnp.float32)


def token_stats_kernel(q_ref, bq_ref, kv_ref, c_ref, bc_ref, stats_ref, bias_ref):
    span = q_ref.shape[0]
    bias_ref[...] = token_bias(span)
    for group in range(KVH):
        keys = kv_ref[:, group * HD : (group + 1) * HD]
        vals = kv_ref[:, (KVH + group) * HD : (KVH + group + 1) * HD]
        for head in range(GROUP + 1):
            query = head_rows(q_ref, bq_ref, group, head)
            cot = head_rows(c_ref, bc_ref, group, head)
            width = query.shape[0]
            scores = dot_nt(keys, query) * (FACTOR * LOG2E)
            if head < GROUP:
                scores = scores + bias_ref[...]
            top = jnp.max(scores, 0, keepdims=True)
            expo = jnp.exp2(scores - top)
            dweights = dot_nt(vals, cot)
            stats_ref[0, group, head : head + 1, :width] = top
            stats_ref[1, group, head : head + 1, :width] = jnp.sum(expo, 0, keepdims=True)
            stats_ref[2, group, head : head + 1, :width] = jnp.sum(
                expo * dweights, 0, keepdims=True
            )


def beacon_grad_kernel(
    pos_ref, q_ref, bq_ref, kv_ref, c_ref, bc_ref, stats_ref, contrib_ref, rows_ref, bias_ref, bbias_ref
):
    total = kv_ref.shape[0]
    span = q_ref.shape[0]
    count = bq_ref.shape[0]
    start = pos_ref[0] * count
    bias_ref[...] = prefix_bias(total, span, start, None)
    bbias_ref[...] = prefix_bias(total, HD, start, count)
    jobs = [(group, head) for group in range(KVH) for head in range(GROUP + 1)]

    def products(group, head):
        query = head_rows(q_ref, bq_ref, group, head)
        cot = head_rows(c_ref, bc_ref, group, head)
        keys = kv_ref[:, group * HD : (group + 1) * HD]
        vals = kv_ref[:, (KVH + group) * HD : (KVH + group + 1) * HD]
        return query, cot, dot_nt(keys, query), dot_nt(vals, cot)

    ahead = products(*jobs[0])
    for at, (group, head) in enumerate(jobs):
        query, cot, scores, dweights = ahead
        if at + 1 < len(jobs):
            ahead = products(*jobs[at + 1])
        if head == 0:
            key_grad = jnp.zeros((total, HD), jnp.float32)
            val_grad = jnp.zeros((total, HD), jnp.float32)
        width = query.shape[0]
        bias = bias_ref if head < GROUP else bbias_ref
        scores = scores * (FACTOR * LOG2E) + bias[...]
        top_tok = stats_ref[0, group, head : head + 1, :width]
        sum_tok = stats_ref[1, group, head : head + 1, :width]
        cen_tok = stats_ref[2, group, head : head + 1, :width]
        top = jnp.maximum(jnp.max(scores, 0, keepdims=True), top_tok)
        shift = jnp.exp2(top_tok - top)
        expo = jnp.exp2(scores - top)
        total_sum = shift * sum_tok + jnp.sum(expo, 0, keepdims=True)
        inverse = 1.0 / total_sum
        centre = inverse * (shift * cen_tok + jnp.sum(expo * dweights, 0, keepdims=True))
        probs = expo * inverse
        dscores = (probs * (dweights - centre)).astype(jnp.bfloat16)
        key_grad = key_grad + dot_nn(dscores, query)
        val_grad = val_grad + dot_nn(probs.astype(jnp.bfloat16), cot)
        rows_ref[0, group, head : head + 1, :width] = top + jnp.log(total_sum) * LOG2E
        rows_ref[1, group, head : head + 1, :width] = centre
        if head == GROUP:
            contrib_ref[:, group * HD : (group + 1) * HD] = (key_grad * FACTOR).astype(jnp.bfloat16)
            contrib_ref[:, (KVH + group) * HD : (KVH + group + 1) * HD] = val_grad.astype(
                jnp.bfloat16
            )


def rest_kernel(
    pos_ref, q_ref, bq_ref, bkv_ref, kv_ref, c_ref, bc_ref, rows_ref,
    out_ref, bout_ref, dq_ref, bdq_ref, dkv_ref, bias_ref, bbias_ref, tbias_ref,
):
    total = bkv_ref.shape[0]
    span = q_ref.shape[0]
    count = bq_ref.shape[0]
    start = pos_ref[0] * count
    bias_ref[...] = prefix_bias(total, span, start, None)
    bbias_ref[...] = prefix_bias(total, HD, start, count)
    tbias_ref[...] = token_bias(span)
    for group in range(KVH):
        key_cols = slice(group * HD, (group + 1) * HD)
        val_cols = slice((KVH + group) * HD, (KVH + group + 1) * HD)
        sides = []
        for ref in (bkv_ref, kv_ref):
            keys = ref[:, key_cols]
            vals = ref[:, val_cols]
            sides.append((keys, vals, keys.T, vals.T))
        key_grad = jnp.zeros((span, HD), jnp.float32)
        val_grad = jnp.zeros((span, HD), jnp.float32)
        for head in range(GROUP + 1):
            query = head_rows(q_ref, bq_ref, group, head)
            cot = head_rows(c_ref, bc_ref, group, head)
            width = query.shape[0]
            lse = rows_ref[0, group, head : head + 1, :width]
            centre = rows_ref[1, group, head : head + 1, :width]
            out = None
            dquery = None
            for side in range(2):
                keys, vals, keys_t, vals_t = sides[side]
                scores = dot_nt(keys, query) * (FACTOR * LOG2E) - lse
                if side == 0:
                    scores = scores + (bias_ref if head < GROUP else bbias_ref)[...]
                elif head < GROUP:
                    scores = scores + tbias_ref[...]
                probs = jnp.exp2(scores)
                dscores = (probs * (dot_nt(vals, cot) - centre)).astype(jnp.bfloat16)
                weights = probs.astype(jnp.bfloat16)
                out_part = dot_nn(vals_t, weights)
                dq_part = dot_nn(keys_t, dscores)
                out = out_part if out is None else out + out_part
                dquery = dq_part if dquery is None else dquery + dq_part
                if side == 1:
                    key_grad = key_grad + dot_nn(dscores, query)
                    val_grad = val_grad + dot_nn(weights, cot)
            out = out.T.astype(jnp.bfloat16)
            dquery = (dquery * FACTOR).T.astype(jnp.bfloat16)
            if head < GROUP:
                at = (group * GROUP + head) * HD
                out_ref[:, at : at + HD] = out
                dq_ref[:, at : at + HD] = dquery
            else:
                for each in range(GROUP):
                    at = (group * GROUP + each) * HD
                    bout_ref[:, at : at + HD] = out[each * count : (each + 1) * count]
                    bdq_ref[:, at : at + HD] = dquery[each * count : (each + 1) * count]
        dkv_ref[:, key_cols] = (key_grad * FACTOR).astype(jnp.bfloat16)
        dkv_ref[:, val_cols] = val_grad.astype(jnp.bfloat16)


VM = pl.BlockSpec(memory_space=pltpu.VMEM)
SM = pl.BlockSpec(memory_space=pltpu.SMEM)


def call(kernel, outs, scratch, specs, args, flops):
    return pl.pallas_call(
        kernel,
        out_shape=outs,
        in_specs=specs,
        out_specs=tuple(VM for _ in outs),
        scratch_shapes=scratch,
        compiler_params=pltpu.CompilerParams(vmem_limit_bytes=40 * 1024 * 1024),
        cost_estimate=pl.CostEstimate(
            flops=flops, bytes_accessed=4 * 1024 * 1024, transcendentals=0
        ),
    )(*args)


def token_stats(query, beacon_query, kv, cot, beacon_cot):
    span = query.shape[0]
    return call(
        token_stats_kernel,
        (jax.ShapeDtypeStruct((3, KVH, GROUP + 1, span), jnp.float32),),
        [pltpu.VMEM((span, span), jnp.float32)],
        [VM] * 5,
        (query, beacon_query, kv, cot, beacon_cot),
        4 * span * span * HD * KVH * (GROUP + 1),
    )[0]


def beacon_grads(pos, query, beacon_query, all_kv, cot, beacon_cot, stats):
    span = query.shape[0]
    total = all_kv.shape[0]
    return call(
        beacon_grad_kernel,
        (
            jax.ShapeDtypeStruct(all_kv.shape, jnp.bfloat16),
            jax.ShapeDtypeStruct((2, KVH, GROUP + 1, span), jnp.float32),
        ),
        [pltpu.VMEM((total, span), jnp.float32), pltpu.VMEM((total, HD), jnp.float32)],
        [SM] + [VM] * 6,
        (pos, query, beacon_query, all_kv, cot, beacon_cot, stats),
        8 * span * total * HD * KVH * (GROUP + 1),
    )


def rest(pos, query, beacon_query, all_kv, kv, cot, beacon_cot, rows):
    span = query.shape[0]
    total = all_kv.shape[0]
    like = lambda x: jax.ShapeDtypeStruct(x.shape, jnp.bfloat16)
    return call(
        rest_kernel,
        (like(query), like(beacon_query), like(query), like(beacon_query), like(kv)),
        [
            pltpu.VMEM((total, span), jnp.float32),
            pltpu.VMEM((total, HD), jnp.float32),
            pltpu.VMEM((span, span), jnp.float32),
        ],
        [SM] + [VM] * 7,
        (pos, query, beacon_query, all_kv, kv, cot, beacon_cot, rows),
        10 * span * (total + span) * HD * KVH * (GROUP + 1),
    )


def hidden_grad_kernel(grad_ref, weight_ref, out_ref):
    part = dot_nt(grad_ref[...], weight_ref[...]).astype(jnp.bfloat16)
    out_ref[...] = part.reshape(out_ref.shape)


def hidden_grad_part(all_grad, weight, count):
    total, width = all_grad.shape
    return call(
        hidden_grad_kernel,
        (jax.ShapeDtypeStruct((count, total // count, weight.shape[0]), jnp.bfloat16),),
        [],
        [VM] * 2,
        (all_grad, weight),
        2 * total * width * weight.shape[0],
    )[0]


def exchange(blocks):
    return lax.all_to_all(blocks, "ctx", 0, 0, tiled=True)


def reduce_blocks(blocks):
    return jnp.sum(exchange(blocks).astype(jnp.float32), 0).astype(jnp.bfloat16)


def gather_rows(rows, count):
    return exchange(jnp.broadcast_to(rows[None], (count,) + rows.shape)).reshape(-1, rows.shape[-1])


def swap_dp(sent, mask):
    pairs = [(i, i ^ mask) for i in range(lax.axis_size("dp"))]
    return lax.ppermute(sent, "dp", pairs).astype(jnp.float32)


def sum_dp(part, beside):
    sent = part.astype(jnp.bfloat16)
    near, far, wide = [swap_dp(sent, mask) for mask in (2, 5, 7)]
    near, far, wide, beside = lax.optimization_barrier((near, far, wide, beside))
    part = (sent.astype(jnp.float32) + near) + (far + wide)
    sent = part.astype(jnp.bfloat16)
    return sent.astype(jnp.float32) + swap_dp(sent, 1), beside


def shards(
    query, keys_values, beacon_query, beacon_hidden, beacon_weight, grad_tokens, grad_beacons
):
    pos = lax.axis_index("ctx").astype(jnp.int32).reshape(1)
    count = lax.axis_size("ctx")
    rows = beacon_hidden.shape[1]
    hidden_rows = beacon_hidden[0]
    stats = token_stats(
        query[0], beacon_query[0], keys_values[0], grad_tokens[0], grad_beacons[0]
    )
    hidden_cols = exchange(hidden_rows.reshape(rows, count, -1).transpose(1, 0, 2))
    hidden_cols = hidden_cols.reshape(rows * count, -1)
    part_kv = jnp.dot(hidden_cols, beacon_weight, preferred_element_type=jnp.float32)
    own_kv = reduce_blocks(part_kv.astype(jnp.bfloat16).reshape(count, rows, -1))
    all_kv = gather_rows(own_kv, count)
    contrib, row_stats = beacon_grads(
        pos, query[0], beacon_query[0], all_kv, grad_tokens[0], grad_beacons[0], stats
    )
    others = rest(
        pos, query[0], beacon_query[0], all_kv, keys_values[0], grad_tokens[0], grad_beacons[0], row_stats
    )
    arrived = exchange(contrib.reshape(count, rows, -1))
    arrived, others = lax.optimization_barrier((arrived, others))
    tokens_out, beacons_out, query_grad, beacon_qgrad, token_kvgrad = others
    own_grad = jnp.sum(arrived.astype(jnp.float32), 0).astype(jnp.bfloat16)
    all_grad = gather_rows(own_grad, count)
    weight_part = lax.dot_general(
        hidden_cols, all_grad, (((0,), (0,)), ((), ())), preferred_element_type=jnp.float32
    )
    hidden_blocks = exchange(hidden_grad_part(all_grad, beacon_weight, count))
    grad_weight, hidden_blocks = sum_dp(weight_part, hidden_blocks)
    hidden_grad = hidden_blocks.transpose(1, 0, 2).reshape(rows, -1)
    return (
        tokens_out[None],
        beacons_out[None],
        query_grad[None],
        token_kvgrad[None],
        beacon_qgrad[None],
        hidden_grad[None],
        grad_weight,
    )


def solution(mesh):
    placed = (
        P("dp", "ctx", None),
        P("dp", "ctx", None),
        P("dp", "ctx", None),
        P("dp", "ctx", None),
        P("ctx", None),
        P("dp", "ctx", None),
        P("dp", "ctx", None),
    )
    return jax.shard_map(
        shards,
        mesh=mesh,
        in_specs=placed,
        out_specs=(
            P("dp", "ctx", None),
            P("dp", "ctx", None),
            P("dp", "ctx", None),
            P("dp", "ctx", None),
            P("dp", "ctx", None),
            P("dp", "ctx", None),
            P("ctx", None),
        ),
        check_vma=False,
    )
```

```python
import jax
import jax.numpy as jnp
from jax import lax
from jax.experimental import pallas as pl
from jax.experimental.pallas import tpu as pltpu
from jax.sharding import PartitionSpec as P

KVH = 2
HD = 128
GROUP = 7
MASKED = -1e30
LOG2E = 1.4426950408889634
FACTOR = HD ** (-0.5)


def dot_nt(left, right):
    return lax.dot_general(
        left, right, (((1,), (1,)), ((), ())), preferred_element_type=jnp.float32
    )


def dot_nn(left, right):
    return jnp.dot(left, right, preferred_element_type=jnp.float32)


def head_rows(tokens_ref, beacons_ref, group, head):
    if head < GROUP:
        start = (group * GROUP + head) * HD
        return tokens_ref[:, start : start + HD]
    parts = []
    for each in range(GROUP):
        start = (group * GROUP + each) * HD
        parts.append(beacons_ref[:, start : start + HD])
    rows = beacons_ref.shape[0]
    parts.append(jnp.zeros((HD - GROUP * rows, HD), beacons_ref.dtype))
    return jnp.concatenate(parts, 0)


def token_bias(span):
    col = lax.broadcasted_iota(jnp.int32, (span, span), 0)
    row = lax.broadcasted_iota(jnp.int32, (span, span), 1)
    return jnp.where(col <= row, 0.0, MASKED).astype(jnp.float32)


def prefix_bias(total, width, start, rank_rows):
    col = lax.broadcasted_iota(jnp.int32, (total, width), 0)
    limit = start
    if rank_rows is not None:
        lane = lax.broadcasted_iota(jnp.int32, (total, width), 1)
        limit = start + 1 + (lane & (rank_rows - 1))
    return jnp.where(col < limit, 0.0, MASKED).astype(jnp.float32)


def token_stats_kernel(q_ref, bq_ref, kv_ref, c_ref, bc_ref, stats_ref, bias_ref):
    span = q_ref.shape[0]
    bias_ref[...] = token_bias(span)
    for group in range(KVH):
        keys = kv_ref[:, group * HD : (group + 1) * HD]
        vals = kv_ref[:, (KVH + group) * HD : (KVH + group + 1) * HD]
        for head in range(GROUP + 1):
            query = head_rows(q_ref, bq_ref, group, head)
            cot = head_rows(c_ref, bc_ref, group, head)
            width = query.shape[0]
            scores = dot_nt(keys, query) * (FACTOR * LOG2E)
            if head < GROUP:
                scores = scores + bias_ref[...]
            top = jnp.max(scores, 0, keepdims=True)
            expo = jnp.exp2(scores - top)
            dweights = dot_nt(vals, cot)
            stats_ref[0, group, head : head + 1, :width] = top
            stats_ref[1, group, head : head + 1, :width] = jnp.sum(expo, 0, keepdims=True)
            stats_ref[2, group, head : head + 1, :width] = jnp.sum(
                expo * dweights, 0, keepdims=True
            )


def beacon_grad_kernel(
    pos_ref, q_ref, bq_ref, kv_ref, c_ref, bc_ref, stats_ref, contrib_ref, rows_ref, bias_ref, bbias_ref
):
    total = kv_ref.shape[0]
    span = q_ref.shape[0]
    count = bq_ref.shape[0]
    start = pos_ref[0] * count
    bias_ref[...] = prefix_bias(total, span, start, None)
    bbias_ref[...] = prefix_bias(total, HD, start, count)
    jobs = [(group, head) for group in range(KVH) for head in range(GROUP + 1)]

    def products(group, head):
        query = head_rows(q_ref, bq_ref, group, head)
        cot = head_rows(c_ref, bc_ref, group, head)
        keys = kv_ref[:, group * HD : (group + 1) * HD]
        vals = kv_ref[:, (KVH + group) * HD : (KVH + group + 1) * HD]
        return query, cot, dot_nt(keys, query), dot_nt(vals, cot)

    ahead = products(*jobs[0])
    for at, (group, head) in enumerate(jobs):
        query, cot, scores, dweights = ahead
        if at + 1 < len(jobs):
            ahead = products(*jobs[at + 1])
        if head == 0:
            key_grad = jnp.zeros((total, HD), jnp.float32)
            val_grad = jnp.zeros((total, HD), jnp.float32)
        width = query.shape[0]
        bias = bias_ref if head < GROUP else bbias_ref
        scores = scores * (FACTOR * LOG2E) + bias[...]
        top_tok = stats_ref[0, group, head : head + 1, :width]
        sum_tok = stats_ref[1, group, head : head + 1, :width]
        cen_tok = stats_ref[2, group, head : head + 1, :width]
        top = jnp.maximum(jnp.max(scores, 0, keepdims=True), top_tok)
        shift = jnp.exp2(top_tok - top)
        expo = jnp.exp2(scores - top)
        total_sum = shift * sum_tok + jnp.sum(expo, 0, keepdims=True)
        inverse = 1.0 / total_sum
        centre = inverse * (shift * cen_tok + jnp.sum(expo * dweights, 0, keepdims=True))
        probs = expo * inverse
        dscores = (probs * (dweights - centre)).astype(jnp.bfloat16)
        key_grad = key_grad + dot_nn(dscores, query)
        val_grad = val_grad + dot_nn(probs.astype(jnp.bfloat16), cot)
        rows_ref[0, group, head : head + 1, :width] = top + jnp.log(total_sum) * LOG2E
        rows_ref[1, group, head : head + 1, :width] = centre
        if head == GROUP:
            contrib_ref[:, group * HD : (group + 1) * HD] = (key_grad * FACTOR).astype(jnp.bfloat16)
            contrib_ref[:, (KVH + group) * HD : (KVH + group + 1) * HD] = val_grad.astype(
                jnp.bfloat16
            )


def rest_kernel(
    pos_ref, q_ref, bq_ref, bkv_ref, kv_ref, c_ref, bc_ref, rows_ref,
    out_ref, bout_ref, dq_ref, bdq_ref, dkv_ref, bias_ref, bbias_ref, tbias_ref,
):
    total = bkv_ref.shape[0]
    span = q_ref.shape[0]
    count = bq_ref.shape[0]
    start = pos_ref[0] * count
    bias_ref[...] = prefix_bias(total, span, start, None)
    bbias_ref[...] = prefix_bias(total, HD, start, count)
    tbias_ref[...] = token_bias(span)
    jobs = [(group, head) for group in range(KVH) for head in range(GROUP + 1)]
    sides = []
    for group in range(KVH):
        key_cols = slice(group * HD, (group + 1) * HD)
        val_cols = slice((KVH + group) * HD, (KVH + group + 1) * HD)
        both = [(ref[:, key_cols], ref[:, val_cols]) for ref in (bkv_ref, kv_ref)]
        sides.append([(keys, vals, keys.T, vals.T) for keys, vals in both])

    def products(group, head):
        query = head_rows(q_ref, bq_ref, group, head)
        cot = head_rows(c_ref, bc_ref, group, head)
        pairs = [(dot_nt(side[0], query), dot_nt(side[1], cot)) for side in sides[group]]
        return query, cot, pairs

    ahead = products(*jobs[0])
    for job, (group, head) in enumerate(jobs):
        query, cot, pairs = ahead
        if job + 1 < len(jobs):
            ahead = products(*jobs[job + 1])
        if head == 0:
            key_grad = jnp.zeros((span, HD), jnp.float32)
            val_grad = jnp.zeros((span, HD), jnp.float32)
        width = query.shape[0]
        lse = rows_ref[0, group, head : head + 1, :width]
        centre = rows_ref[1, group, head : head + 1, :width]
        out = jnp.zeros((HD, width), jnp.float32)
        dquery = jnp.zeros((HD, width), jnp.float32)
        for side in range(2):
            _, _, keys_t, vals_t = sides[group][side]
            scores = pairs[side][0] * (FACTOR * LOG2E) - lse
            if side == 0:
                scores = scores + (bias_ref if head < GROUP else bbias_ref)[...]
            elif head < GROUP:
                scores = scores + tbias_ref[...]
            probs = jnp.exp2(scores)
            dscores = (probs * (pairs[side][1] - centre)).astype(jnp.bfloat16)
            weights = probs.astype(jnp.bfloat16)
            out = out + dot_nn(vals_t, weights)
            dquery = dquery + dot_nn(keys_t, dscores)
            if side == 1:
                key_grad = key_grad + dot_nn(dscores, query)
                val_grad = val_grad + dot_nn(weights, cot)
        out = out.T.astype(jnp.bfloat16)
        dquery = (dquery * FACTOR).T.astype(jnp.bfloat16)
        if head < GROUP:
            at = (group * GROUP + head) * HD
            out_ref[:, at : at + HD] = out
            dq_ref[:, at : at + HD] = dquery
            continue
        for each in range(GROUP):
            at = (group * GROUP + each) * HD
            bout_ref[:, at : at + HD] = out[each * count : (each + 1) * count]
            bdq_ref[:, at : at + HD] = dquery[each * count : (each + 1) * count]
        dkv_ref[:, group * HD : (group + 1) * HD] = (key_grad * FACTOR).astype(jnp.bfloat16)
        dkv_ref[:, (KVH + group) * HD : (KVH + group + 1) * HD] = val_grad.astype(jnp.bfloat16)


VM = pl.BlockSpec(memory_space=pltpu.VMEM)
SM = pl.BlockSpec(memory_space=pltpu.SMEM)


def call(kernel, outs, scratch, specs, args, flops):
    return pl.pallas_call(
        kernel,
        out_shape=outs,
        in_specs=specs,
        out_specs=tuple(VM for _ in outs),
        scratch_shapes=scratch,
        compiler_params=pltpu.CompilerParams(vmem_limit_bytes=40 * 1024 * 1024),
        cost_estimate=pl.CostEstimate(
            flops=flops, bytes_accessed=4 * 1024 * 1024, transcendentals=0
        ),
    )(*args)


def token_stats(query, beacon_query, kv, cot, beacon_cot):
    span = query.shape[0]
    return call(
        token_stats_kernel,
        (jax.ShapeDtypeStruct((3, KVH, GROUP + 1, span), jnp.float32),),
        [pltpu.VMEM((span, span), jnp.float32)],
        [VM] * 5,
        (query, beacon_query, kv, cot, beacon_cot),
        4 * span * span * HD * KVH * (GROUP + 1),
    )[0]


def beacon_grads(pos, query, beacon_query, all_kv, cot, beacon_cot, stats):
    span = query.shape[0]
    total = all_kv.shape[0]
    return call(
        beacon_grad_kernel,
        (
            jax.ShapeDtypeStruct(all_kv.shape, jnp.bfloat16),
            jax.ShapeDtypeStruct((2, KVH, GROUP + 1, span), jnp.float32),
        ),
        [pltpu.VMEM((total, span), jnp.float32), pltpu.VMEM((total, HD), jnp.float32)],
        [SM] + [VM] * 6,
        (pos, query, beacon_query, all_kv, cot, beacon_cot, stats),
        8 * span * total * HD * KVH * (GROUP + 1),
    )


def rest(pos, query, beacon_query, all_kv, kv, cot, beacon_cot, rows):
    span = query.shape[0]
    total = all_kv.shape[0]
    like = lambda x: jax.ShapeDtypeStruct(x.shape, jnp.bfloat16)
    return call(
        rest_kernel,
        (like(query), like(beacon_query), like(query), like(beacon_query), like(kv)),
        [
            pltpu.VMEM((total, span), jnp.float32),
            pltpu.VMEM((total, HD), jnp.float32),
            pltpu.VMEM((span, span), jnp.float32),
        ],
        [SM] + [VM] * 7,
        (pos, query, beacon_query, all_kv, kv, cot, beacon_cot, rows),
        10 * span * (total + span) * HD * KVH * (GROUP + 1),
    )


def hidden_grad_kernel(grad_ref, weight_ref, out_ref):
    part = dot_nt(grad_ref[...], weight_ref[...]).astype(jnp.bfloat16)
    out_ref[...] = part.reshape(out_ref.shape)


def hidden_grad_part(all_grad, weight, count):
    total, width = all_grad.shape
    return call(
        hidden_grad_kernel,
        (jax.ShapeDtypeStruct((count, total // count, weight.shape[0]), jnp.bfloat16),),
        [],
        [VM] * 2,
        (all_grad, weight),
        2 * total * width * weight.shape[0],
    )[0]


def weight_grad_kernel(hidden_ref, grad_ref, out_ref):
    rows = grad_ref.shape[0]
    out_ref[...] = lax.dot_general(
        hidden_ref[...].reshape(rows, -1),
        grad_ref[...],
        (((0,), (0,)), ((), ())),
        preferred_element_type=jnp.float32,
    ).astype(jnp.bfloat16)


def weight_grad_part(hidden_blocks, all_grad):
    return call(
        weight_grad_kernel,
        (jax.ShapeDtypeStruct((hidden_blocks.shape[-1], all_grad.shape[1]), jnp.bfloat16),),
        [],
        [VM] * 2,
        (hidden_blocks, all_grad),
        10**10,
    )[0]


def exchange(blocks):
    return lax.all_to_all(blocks, "ctx", 0, 0, tiled=True)


def reduce_blocks(blocks):
    return jnp.sum(exchange(blocks).astype(jnp.float32), 0).astype(jnp.bfloat16)


def gather_rows(rows, count):
    return exchange(jnp.broadcast_to(rows[None], (count,) + rows.shape)).reshape(-1, rows.shape[-1])


def swap_dp(sent, mask):
    pairs = [(i, i ^ mask) for i in range(lax.axis_size("dp"))]
    return lax.ppermute(sent, "dp", pairs).astype(jnp.float32)


def sum_dp(part, beside):
    sent = part
    near, far, wide = [swap_dp(sent, mask) for mask in (2, 5, 7)]
    sent, beside = lax.optimization_barrier((sent, beside))
    part = (sent.astype(jnp.float32) + near) + (far + wide)
    sent = part.astype(jnp.bfloat16)
    return sent.astype(jnp.float32) + swap_dp(sent, 1), beside


def shards(
    query, keys_values, beacon_query, beacon_hidden, beacon_weight, grad_tokens, grad_beacons
):
    pos = lax.axis_index("ctx").astype(jnp.int32).reshape(1)
    count = lax.axis_size("ctx")
    rows = beacon_hidden.shape[1]
    hidden_rows = beacon_hidden[0]
    stats = token_stats(
        query[0], beacon_query[0], keys_values[0], grad_tokens[0], grad_beacons[0]
    )
    hidden_cols = exchange(hidden_rows.reshape(rows, count, -1).transpose(1, 0, 2))
    hidden_cols = hidden_cols.reshape(rows * count, -1)
    part_kv = jnp.dot(hidden_cols, beacon_weight, preferred_element_type=jnp.float32)
    own_kv = reduce_blocks(part_kv.astype(jnp.bfloat16).reshape(count, rows, -1))
    all_kv = gather_rows(own_kv, count)
    contrib, row_stats = beacon_grads(
        pos, query[0], beacon_query[0], all_kv, grad_tokens[0], grad_beacons[0], stats
    )
    others = rest(
        pos, query[0], beacon_query[0], all_kv, keys_values[0], grad_tokens[0], grad_beacons[0], row_stats
    )
    arrived = exchange(contrib.reshape(count, rows, -1))
    arrived, others = lax.optimization_barrier((arrived, others))
    tokens_out, beacons_out, query_grad, beacon_qgrad, token_kvgrad = others
    own_grad = jnp.sum(arrived.astype(jnp.float32), 0).astype(jnp.bfloat16)
    all_grad = gather_rows(own_grad, count)
    hidden_part = hidden_grad_part(all_grad, beacon_weight, count)
    hidden_part, late_grad = lax.optimization_barrier((hidden_part, all_grad))
    weight_part = weight_grad_part(hidden_cols, late_grad)
    hidden_blocks = exchange(hidden_part)
    grad_weight, hidden_blocks = sum_dp(weight_part, hidden_blocks)
    hidden_grad = hidden_blocks.transpose(1, 0, 2).reshape(rows, -1)
    return (
        tokens_out[None],
        beacons_out[None],
        query_grad[None],
        token_kvgrad[None],
        beacon_qgrad[None],
        hidden_grad[None],
        grad_weight,
    )


def solution(mesh):
    placed = (
        P("dp", "ctx", None),
        P("dp", "ctx", None),
        P("dp", "ctx", None),
        P("dp", "ctx", None),
        P("ctx", None),
        P("dp", "ctx", None),
        P("dp", "ctx", None),
    )
    return jax.shard_map(
        shards,
        mesh=mesh,
        in_specs=placed,
        out_specs=(
            P("dp", "ctx", None),
            P("dp", "ctx", None),
            P("dp", "ctx", None),
            P("dp", "ctx", None),
            P("dp", "ctx", None),
            P("dp", "ctx", None),
            P("ctx", None),
        ),
        check_vma=False,
    )
```

```python
import jax
import jax.numpy as jnp
from jax import lax
from jax.experimental import pallas as pl
from jax.experimental.pallas import tpu as pltpu
from jax.sharding import PartitionSpec as P

KVH = 2
HD = 128
GROUP = 7
LINES = 4
MASKED = -1e30
LOG2E = 1.4426950408889634
FACTOR = HD ** (-0.5)


def dot_nt(left, right):
    return lax.dot_general(
        left, right, (((1,), (1,)), ((), ())), preferred_element_type=jnp.float32
    )


def dot_nn(left, right):
    return jnp.dot(left, right, preferred_element_type=jnp.float32)


def head_rows(tokens_ref, beacons_ref, group, head):
    if head < GROUP:
        start = (group * GROUP + head) * HD
        return tokens_ref[:, start : start + HD]
    parts = []
    for each in range(GROUP):
        start = (group * GROUP + each) * HD
        parts.append(beacons_ref[:, start : start + HD])
    rows = beacons_ref.shape[0]
    parts.append(jnp.zeros((HD - GROUP * rows, HD), beacons_ref.dtype))
    return jnp.concatenate(parts, 0)


def token_bias(span):
    col = lax.broadcasted_iota(jnp.int32, (span, span), 0)
    row = lax.broadcasted_iota(jnp.int32, (span, span), 1)
    return jnp.where(col <= row, 0.0, MASKED).astype(jnp.float32)


def prefix_bias(total, width, start, rank_rows):
    col = lax.broadcasted_iota(jnp.int32, (total, width), 0)
    limit = start
    if rank_rows is not None:
        lane = lax.broadcasted_iota(jnp.int32, (total, width), 1)
        limit = start + 1 + (lane & (rank_rows - 1))
    return jnp.where(col < limit, 0.0, MASKED).astype(jnp.float32)


def token_stats_kernel(q_ref, bq_ref, kv_ref, c_ref, bc_ref, stats_ref, bias_ref):
    span = q_ref.shape[0]
    bias_ref[...] = token_bias(span)
    for group in range(KVH):
        keys = kv_ref[:, group * HD : (group + 1) * HD]
        vals = kv_ref[:, (KVH + group) * HD : (KVH + group + 1) * HD]
        for head in range(GROUP + 1):
            query = head_rows(q_ref, bq_ref, group, head)
            cot = head_rows(c_ref, bc_ref, group, head)
            width = query.shape[0]
            scores = dot_nt(keys, query) * (FACTOR * LOG2E)
            if head < GROUP:
                scores = scores + bias_ref[...]
            top = jnp.max(scores, 0, keepdims=True)
            expo = jnp.exp2(scores - top)
            dweights = dot_nt(vals, cot)
            stats_ref[0, group, head : head + 1, :width] = top
            stats_ref[1, group, head : head + 1, :width] = jnp.sum(expo, 0, keepdims=True)
            stats_ref[2, group, head : head + 1, :width] = jnp.sum(
                expo * dweights, 0, keepdims=True
            )


def beacon_grad_kernel(
    pos_ref, q_ref, bq_ref, kv_ref, c_ref, bc_ref, stats_ref, contrib_ref, rows_ref, bias_ref, bbias_ref
):
    total = kv_ref.shape[0]
    span = q_ref.shape[0]
    count = bq_ref.shape[0]
    start = pos_ref[0] * count
    bias_ref[...] = prefix_bias(total, span, start, None)
    bbias_ref[...] = prefix_bias(total, HD, start, count)
    jobs = [(group, head) for group in range(KVH) for head in range(GROUP + 1)]

    def products(group, head):
        query = head_rows(q_ref, bq_ref, group, head)
        cot = head_rows(c_ref, bc_ref, group, head)
        keys = kv_ref[:, group * HD : (group + 1) * HD]
        vals = kv_ref[:, (KVH + group) * HD : (KVH + group + 1) * HD]
        return query, cot, dot_nt(keys, query), dot_nt(vals, cot)

    ahead = products(*jobs[0])
    for at, (group, head) in enumerate(jobs):
        query, cot, scores, dweights = ahead
        if at + 1 < len(jobs):
            ahead = products(*jobs[at + 1])
        if head == 0:
            key_grad = jnp.zeros((total, HD), jnp.float32)
            val_grad = jnp.zeros((total, HD), jnp.float32)
        width = query.shape[0]
        bias = bias_ref if head < GROUP else bbias_ref
        scores = scores * (FACTOR * LOG2E) + bias[...]
        top_tok = stats_ref[0, group, head : head + 1, :width]
        sum_tok = stats_ref[1, group, head : head + 1, :width]
        cen_tok = stats_ref[2, group, head : head + 1, :width]
        top = jnp.maximum(jnp.max(scores, 0, keepdims=True), top_tok)
        shift = jnp.exp2(top_tok - top)
        expo = jnp.exp2(scores - top)
        total_sum = shift * sum_tok + jnp.sum(expo, 0, keepdims=True)
        inverse = 1.0 / total_sum
        centre = inverse * (shift * cen_tok + jnp.sum(expo * dweights, 0, keepdims=True))
        probs = expo * inverse
        dscores = (probs * (dweights - centre)).astype(jnp.bfloat16)
        key_grad = key_grad + dot_nn(dscores, query)
        val_grad = val_grad + dot_nn(probs.astype(jnp.bfloat16), cot)
        rows_ref[0, group, head : head + 1, :width] = top + jnp.log(total_sum) * LOG2E
        rows_ref[1, group, head : head + 1, :width] = centre
        if head == GROUP:
            contrib_ref[:, group * HD : (group + 1) * HD] = (key_grad * FACTOR).astype(jnp.bfloat16)
            contrib_ref[:, (KVH + group) * HD : (KVH + group + 1) * HD] = val_grad.astype(
                jnp.bfloat16
            )


def rest_kernel(
    pos_ref, q_ref, bq_ref, bkv_ref, kv_ref, c_ref, bc_ref, rows_ref,
    out_ref, bout_ref, dq_ref, bdq_ref, dkv_ref, bias_ref, bbias_ref, tbias_ref,
):
    total = bkv_ref.shape[0]
    span = q_ref.shape[0]
    count = bq_ref.shape[0]
    start = pos_ref[0] * count
    bias_ref[...] = prefix_bias(total, span, start, None)
    bbias_ref[...] = prefix_bias(total, HD, start, count)
    tbias_ref[...] = token_bias(span)
    jobs = [(group, head) for group in range(KVH) for head in range(GROUP + 1)]
    sides = []
    for group in range(KVH):
        key_cols = slice(group * HD, (group + 1) * HD)
        val_cols = slice((KVH + group) * HD, (KVH + group + 1) * HD)
        both = [(ref[:, key_cols], ref[:, val_cols]) for ref in (bkv_ref, kv_ref)]
        sides.append([(keys, vals, keys.T, vals.T) for keys, vals in both])

    def products(group, head):
        query = head_rows(q_ref, bq_ref, group, head)
        cot = head_rows(c_ref, bc_ref, group, head)
        pairs = [(dot_nt(side[0], query), dot_nt(side[1], cot)) for side in sides[group]]
        return query, cot, pairs

    ahead = products(*jobs[0])
    for job, (group, head) in enumerate(jobs):
        query, cot, pairs = ahead
        if job + 1 < len(jobs):
            ahead = products(*jobs[job + 1])
        if head == 0:
            key_grad = jnp.zeros((span, HD), jnp.float32)
            val_grad = jnp.zeros((span, HD), jnp.float32)
        width = query.shape[0]
        lse = rows_ref[0, group, head : head + 1, :width]
        centre = rows_ref[1, group, head : head + 1, :width]
        out = jnp.zeros((HD, width), jnp.float32)
        dquery = jnp.zeros((HD, width), jnp.float32)
        for side in range(2):
            _, _, keys_t, vals_t = sides[group][side]
            scores = pairs[side][0] * (FACTOR * LOG2E) - lse
            if side == 0:
                scores = scores + (bias_ref if head < GROUP else bbias_ref)[...]
            elif head < GROUP:
                scores = scores + tbias_ref[...]
            probs = jnp.exp2(scores)
            dscores = (probs * (pairs[side][1] - centre)).astype(jnp.bfloat16)
            weights = probs.astype(jnp.bfloat16)
            out = out + dot_nn(vals_t, weights)
            dquery = dquery + dot_nn(keys_t, dscores)
            if side == 1:
                key_grad = key_grad + dot_nn(dscores, query)
                val_grad = val_grad + dot_nn(weights, cot)
        out = out.T.astype(jnp.bfloat16)
        dquery = (dquery * FACTOR).T.astype(jnp.bfloat16)
        if head < GROUP:
            at = (group * GROUP + head) * HD
            out_ref[:, at : at + HD] = out
            dq_ref[:, at : at + HD] = dquery
            continue
        for each in range(GROUP):
            at = (group * GROUP + each) * HD
            bout_ref[:, at : at + HD] = out[each * count : (each + 1) * count]
            bdq_ref[:, at : at + HD] = dquery[each * count : (each + 1) * count]
        dkv_ref[:, group * HD : (group + 1) * HD] = (key_grad * FACTOR).astype(jnp.bfloat16)
        dkv_ref[:, (KVH + group) * HD : (KVH + group + 1) * HD] = val_grad.astype(jnp.bfloat16)


VM = pl.BlockSpec(memory_space=pltpu.VMEM)
SM = pl.BlockSpec(memory_space=pltpu.SMEM)


def call(kernel, outs, scratch, specs, args, flops):
    return pl.pallas_call(
        kernel,
        out_shape=outs,
        in_specs=specs,
        out_specs=tuple(VM for _ in outs),
        scratch_shapes=scratch,
        compiler_params=pltpu.CompilerParams(vmem_limit_bytes=16 * 1024 * 1024),
        cost_estimate=pl.CostEstimate(
            flops=flops, bytes_accessed=4 * 1024 * 1024, transcendentals=0
        ),
    )(*args)


def token_stats(query, beacon_query, kv, cot, beacon_cot):
    span = query.shape[0]
    return call(
        token_stats_kernel,
        (jax.ShapeDtypeStruct((3, KVH, GROUP + 1, span), jnp.float32),),
        [pltpu.VMEM((span, span), jnp.float32)],
        [VM] * 5,
        (query, beacon_query, kv, cot, beacon_cot),
        4 * span * span * HD * KVH * (GROUP + 1),
    )[0]


def beacon_grads(pos, query, beacon_query, all_kv, cot, beacon_cot, stats):
    span = query.shape[0]
    total = all_kv.shape[0]
    return call(
        beacon_grad_kernel,
        (
            jax.ShapeDtypeStruct(all_kv.shape, jnp.bfloat16),
            jax.ShapeDtypeStruct((2, KVH, GROUP + 1, span), jnp.float32),
        ),
        [pltpu.VMEM((total, span), jnp.float32), pltpu.VMEM((total, HD), jnp.float32)],
        [SM] + [VM] * 6,
        (pos, query, beacon_query, all_kv, cot, beacon_cot, stats),
        8 * span * total * HD * KVH * (GROUP + 1),
    )


def rest(pos, query, beacon_query, all_kv, kv, cot, beacon_cot, rows):
    span = query.shape[0]
    total = all_kv.shape[0]
    like = lambda x: jax.ShapeDtypeStruct(x.shape, jnp.bfloat16)
    return call(
        rest_kernel,
        (like(query), like(beacon_query), like(query), like(beacon_query), like(kv)),
        [
            pltpu.VMEM((total, span), jnp.float32),
            pltpu.VMEM((total, HD), jnp.float32),
            pltpu.VMEM((span, span), jnp.float32),
        ],
        [SM] + [VM] * 7,
        (pos, query, beacon_query, all_kv, kv, cot, beacon_cot, rows),
        10 * span * (total + span) * HD * KVH * (GROUP + 1),
    )


def partial_kernel(line_ref, hidden_ref, w0_ref, w1_ref, w2_ref, w3_ref, part_ref, *block_refs):
    line = line_ref[0]
    rows = hidden_ref.shape[0] * hidden_ref.shape[2]
    total = jnp.zeros((rows, w0_ref.shape[1]), jnp.float32)
    for step, w_ref in enumerate((w0_ref, w1_ref, w2_ref, w3_ref)):
        block = hidden_ref[:, line ^ step].reshape(rows, w_ref.shape[0])
        block_refs[step][...] = block
        total = total + dot_nn(block, w_ref[...])
    part_ref[...] = total.astype(jnp.bfloat16).reshape(part_ref.shape)


def partial_kv(line, hidden, weights):
    size, _, rows, depth = hidden.shape
    block = jax.ShapeDtypeStruct((size * rows, depth), jnp.bfloat16)
    part = jax.ShapeDtypeStruct((size, rows, weights[0].shape[1]), jnp.bfloat16)
    return call(
        partial_kernel,
        (part,) + (block,) * LINES,
        [],
        [SM] + [VM] * (1 + LINES),
        (line, hidden) + tuple(weights),
        2 * LINES * size * rows * depth * weights[0].shape[1],
    )


def hidden_grad_kernel(line_ref, grad_ref, w0_ref, w1_ref, w2_ref, w3_ref, out_ref):
    line = line_ref[0]
    rows = grad_ref.shape[0] // LINES
    grad = grad_ref[pl.ds(pl.multiple_of(line * rows, rows), rows), :]
    for step, w_ref in enumerate((w0_ref, w1_ref, w2_ref, w3_ref)):
        part = dot_nt(grad, w_ref[...]).astype(jnp.bfloat16)
        out_ref[:, line ^ step] = part.reshape(out_ref.shape[0], out_ref.shape[2], -1)


def hidden_grad_part(line, all_grad, weights, size):
    total, width = all_grad.shape
    depth = weights[0].shape[0]
    return call(
        hidden_grad_kernel,
        (jax.ShapeDtypeStruct((size, LINES, total // (LINES * size), depth), jnp.bfloat16),),
        [],
        [SM] + [VM] * (1 + LINES),
        (line, all_grad) + tuple(weights),
        2 * total * width * depth,
    )[0]


def weight_grad_kernel(line_ref, grad_ref, h0_ref, h1_ref, h2_ref, h3_ref, out_ref):
    line = line_ref[0]
    rows = grad_ref.shape[0] // LINES
    total = jnp.zeros(out_ref.shape, jnp.float32)
    for step, h_ref in enumerate((h0_ref, h1_ref, h2_ref, h3_ref)):
        at = pl.multiple_of((line ^ step) * rows, rows)
        total = total + lax.dot_general(
            h_ref[...],
            grad_ref[pl.ds(at, rows), :],
            (((0,), (0,)), ((), ())),
            preferred_element_type=jnp.float32,
        )
    out_ref[...] = total.astype(jnp.bfloat16)


def weight_grad_part(line, all_grad, hiddens):
    return call(
        weight_grad_kernel,
        (jax.ShapeDtypeStruct((hiddens[0].shape[1], all_grad.shape[1]), jnp.bfloat16),),
        [],
        [SM] + [VM] * (1 + LINES),
        (line, all_grad) + tuple(hiddens),
        10**9,
    )[0]


def sum_kernel(arrived_ref, spread_ref):
    own = jnp.sum(arrived_ref[...].astype(jnp.float32), 0).astype(jnp.bfloat16)
    spread_ref[...] = jnp.broadcast_to(own[None], spread_ref.shape)


def sum_and_spread(arrived):
    shape = jax.ShapeDtypeStruct(arrived.shape, jnp.bfloat16)
    return call(sum_kernel, (shape,), [], [VM], (arrived,), 1024)[0]


def exchange(blocks):
    return lax.all_to_all(blocks, "ctx", 0, 0, tiled=True)


def exchange_line(blocks):
    size = blocks.shape[0]
    groups = [[line * size + i for i in range(size)] for line in range(LINES)]
    return lax.all_to_all(blocks, "ctx", 0, 0, axis_index_groups=groups, tiled=True)


def swap(rows, axis, mask):
    pairs = [(i, i ^ mask) for i in range(lax.axis_size(axis))]
    return lax.ppermute(rows, axis, pairs)


def sum_dp(sent, beside):
    near, far, wide = [swap(sent, "dp", mask).astype(jnp.float32) for mask in (2, 5, 7)]
    sent, beside = lax.optimization_barrier((sent, beside))
    sent = ((sent.astype(jnp.float32) + near) + (far + wide)).astype(jnp.bfloat16)
    return sent.astype(jnp.float32) + swap(sent, "dp", 1).astype(jnp.float32), beside


def shards(
    query, keys_values, beacon_query, beacon_hidden, beacon_weight, grad_tokens, grad_beacons
):
    count = lax.axis_size("ctx")
    size = count // LINES
    index = lax.axis_index("ctx").astype(jnp.int32)
    pos = index.reshape(1)
    line = (index // size).reshape(1)
    rows = beacon_hidden.shape[1]
    stats = token_stats(
        query[0], beacon_query[0], keys_values[0], grad_tokens[0], grad_beacons[0]
    )

    hidden = beacon_hidden[0].reshape(rows, LINES, size, -1).transpose(2, 1, 0, 3)
    hidden, late_weight = lax.optimization_barrier((hidden, beacon_weight))
    hidden = exchange_line(hidden)
    weights = [beacon_weight] + [
        swap(late_weight, "ctx", step * size) for step in range(1, LINES)
    ]
    part_kv, *blocks = partial_kv(line, hidden, weights)
    own_kv = jnp.sum(exchange_line(part_kv).astype(jnp.float32), 0).astype(jnp.bfloat16)
    all_kv = exchange(jnp.broadcast_to(own_kv[None], (count,) + own_kv.shape))
    all_kv = all_kv.reshape(rows * count, -1)
    columns = [blocks[0]] + [
        swap(blocks[step], "ctx", step * size) for step in range(1, LINES)
    ]

    contrib, row_stats = beacon_grads(
        pos, query[0], beacon_query[0], all_kv, grad_tokens[0], grad_beacons[0], stats
    )
    others = rest(
        pos, query[0], beacon_query[0], all_kv, keys_values[0], grad_tokens[0], grad_beacons[0], row_stats
    )
    arrived = exchange(contrib.reshape(count, rows, -1))
    arrived, others = lax.optimization_barrier((arrived, others))
    tokens_out, beacons_out, query_grad, beacon_qgrad, token_kvgrad = others
    all_grad = exchange(sum_and_spread(arrived)).reshape(rows * count, -1)

    hidden_part = hidden_grad_part(line, all_grad, weights, size)
    hidden_part, late_grad = lax.optimization_barrier((hidden_part, all_grad))
    weight_part = weight_grad_part(line, late_grad, columns)
    hidden_blocks = exchange_line(hidden_part)
    grad_weight, hidden_blocks = sum_dp(weight_part, hidden_blocks)
    hidden_grad = hidden_blocks.transpose(2, 1, 0, 3).reshape(rows, -1)
    return (
        tokens_out[None],
        beacons_out[None],
        query_grad[None],
        token_kvgrad[None],
        beacon_qgrad[None],
        hidden_grad[None],
        grad_weight,
    )


def solution(mesh):
    placed = (
        P("dp", "ctx", None),
        P("dp", "ctx", None),
        P("dp", "ctx", None),
        P("dp", "ctx", None),
        P("ctx", None),
        P("dp", "ctx", None),
        P("dp", "ctx", None),
    )
    return jax.shard_map(
        shards,
        mesh=mesh,
        in_specs=placed,
        out_specs=(
            P("dp", "ctx", None),
            P("dp", "ctx", None),
            P("dp", "ctx", None),
            P("dp", "ctx", None),
            P("dp", "ctx", None),
            P("dp", "ctx", None),
            P("ctx", None),
        ),
        check_vma=False,
    )
```

```python
import functools

import jax
import jax.numpy as jnp
from jax import lax
from jax.experimental import pallas as pl
from jax.experimental.pallas import tpu as pltpu
from jax.sharding import PartitionSpec as P

KVH = 2
HD = 128
GROUP = 7
LINES = 4
MASKED = -1e30
LOG2E = 1.4426950408889634
FACTOR = HD ** (-0.5)


def dot_nt(left, right):
    return lax.dot_general(
        left, right, (((1,), (1,)), ((), ())), preferred_element_type=jnp.float32
    )


def dot_nn(left, right):
    return jnp.dot(left, right, preferred_element_type=jnp.float32)


def head_rows(tokens_ref, beacons_ref, group, head):
    if head < GROUP:
        start = (group * GROUP + head) * HD
        return tokens_ref[:, start : start + HD]
    parts = []
    for each in range(GROUP):
        start = (group * GROUP + each) * HD
        parts.append(beacons_ref[:, start : start + HD])
    rows = beacons_ref.shape[0]
    parts.append(jnp.zeros((HD - GROUP * rows, HD), beacons_ref.dtype))
    return jnp.concatenate(parts, 0)


def token_bias(span):
    col = lax.broadcasted_iota(jnp.int32, (span, span), 0)
    row = lax.broadcasted_iota(jnp.int32, (span, span), 1)
    return jnp.where(col <= row, 0.0, MASKED).astype(jnp.float32)


def prefix_bias(total, width, start, rank_rows):
    col = lax.broadcasted_iota(jnp.int32, (total, width), 0)
    limit = start
    if rank_rows is not None:
        lane = lax.broadcasted_iota(jnp.int32, (total, width), 1)
        limit = start + 1 + (lane & (rank_rows - 1))
    return jnp.where(col < limit, 0.0, MASKED).astype(jnp.float32)


def token_stats_kernel(q_ref, bq_ref, kv_ref, c_ref, bc_ref, stats_ref, bias_ref):
    span = q_ref.shape[0]
    bias_ref[...] = token_bias(span)
    for group in range(KVH):
        keys = kv_ref[:, group * HD : (group + 1) * HD]
        vals = kv_ref[:, (KVH + group) * HD : (KVH + group + 1) * HD]
        for head in range(GROUP + 1):
            query = head_rows(q_ref, bq_ref, group, head)
            cot = head_rows(c_ref, bc_ref, group, head)
            width = query.shape[0]
            scores = dot_nt(keys, query) * (FACTOR * LOG2E)
            if head < GROUP:
                scores = scores + bias_ref[...]
            top = jnp.max(scores, 0, keepdims=True)
            expo = jnp.exp2(scores - top)
            dweights = dot_nt(vals, cot)
            stats_ref[0, group, head : head + 1, :width] = top
            stats_ref[1, group, head : head + 1, :width] = jnp.sum(expo, 0, keepdims=True)
            stats_ref[2, group, head : head + 1, :width] = jnp.sum(
                expo * dweights, 0, keepdims=True
            )


def beacon_grad_kernel(
    pos_ref, q_ref, bq_ref, kv_ref, c_ref, bc_ref, stats_ref, contrib_ref, rows_ref, bias_ref, bbias_ref
):
    total = kv_ref.shape[0]
    span = q_ref.shape[0]
    count = bq_ref.shape[0]
    start = pos_ref[0] * count
    bias_ref[...] = prefix_bias(total, span, start, None)
    bbias_ref[...] = prefix_bias(total, HD, start, count)
    jobs = [(group, head) for group in range(KVH) for head in range(GROUP + 1)]

    def products(group, head):
        query = head_rows(q_ref, bq_ref, group, head)
        cot = head_rows(c_ref, bc_ref, group, head)
        keys = kv_ref[:, group * HD : (group + 1) * HD]
        vals = kv_ref[:, (KVH + group) * HD : (KVH + group + 1) * HD]
        return query, cot, dot_nt(keys, query), dot_nt(vals, cot)

    ahead = products(*jobs[0])
    for at, (group, head) in enumerate(jobs):
        query, cot, scores, dweights = ahead
        if at + 1 < len(jobs):
            ahead = products(*jobs[at + 1])
        if head == 0:
            key_grad = jnp.zeros((total, HD), jnp.float32)
            val_grad = jnp.zeros((total, HD), jnp.float32)
        width = query.shape[0]
        bias = bias_ref if head < GROUP else bbias_ref
        scores = scores * (FACTOR * LOG2E) + bias[...]
        top_tok = stats_ref[0, group, head : head + 1, :width]
        sum_tok = stats_ref[1, group, head : head + 1, :width]
        cen_tok = stats_ref[2, group, head : head + 1, :width]
        top = jnp.maximum(jnp.max(scores, 0, keepdims=True), top_tok)
        shift = jnp.exp2(top_tok - top)
        expo = jnp.exp2(scores - top)
        total_sum = shift * sum_tok + jnp.sum(expo, 0, keepdims=True)
        inverse = 1.0 / total_sum
        centre = inverse * (shift * cen_tok + jnp.sum(expo * dweights, 0, keepdims=True))
        probs = expo * inverse
        dscores = (probs * (dweights - centre)).astype(jnp.bfloat16)
        key_grad = key_grad + dot_nn(dscores, query)
        val_grad = val_grad + dot_nn(probs.astype(jnp.bfloat16), cot)
        rows_ref[0, group, head : head + 1, :width] = top + jnp.log(total_sum) * LOG2E
        rows_ref[1, group, head : head + 1, :width] = centre
        if head == GROUP:
            contrib_ref[:, group * HD : (group + 1) * HD] = (key_grad * FACTOR).astype(jnp.bfloat16)
            contrib_ref[:, (KVH + group) * HD : (KVH + group + 1) * HD] = val_grad.astype(
                jnp.bfloat16
            )


def rest_kernel(
    pos_ref, q_ref, bq_ref, bkv_ref, kv_ref, c_ref, bc_ref, rows_ref,
    out_ref, bout_ref, dq_ref, bdq_ref, dkv_ref, bias_ref, bbias_ref, tbias_ref,
):
    total = bkv_ref.shape[0]
    span = q_ref.shape[0]
    count = bq_ref.shape[0]
    start = pos_ref[0] * count
    bias_ref[...] = prefix_bias(total, span, start, None)
    bbias_ref[...] = prefix_bias(total, HD, start, count)
    tbias_ref[...] = token_bias(span)
    jobs = [(group, head) for group in range(KVH) for head in range(GROUP + 1)]
    sides = []
    for group in range(KVH):
        key_cols = slice(group * HD, (group + 1) * HD)
        val_cols = slice((KVH + group) * HD, (KVH + group + 1) * HD)
        both = [(ref[:, key_cols], ref[:, val_cols]) for ref in (bkv_ref, kv_ref)]
        sides.append([(keys, vals, keys.T, vals.T) for keys, vals in both])

    def products(group, head):
        query = head_rows(q_ref, bq_ref, group, head)
        cot = head_rows(c_ref, bc_ref, group, head)
        pairs = [(dot_nt(side[0], query), dot_nt(side[1], cot)) for side in sides[group]]
        return query, cot, pairs

    ahead = products(*jobs[0])
    for job, (group, head) in enumerate(jobs):
        query, cot, pairs = ahead
        if job + 1 < len(jobs):
            ahead = products(*jobs[job + 1])
        if head == 0:
            key_grad = jnp.zeros((span, HD), jnp.float32)
            val_grad = jnp.zeros((span, HD), jnp.float32)
        width = query.shape[0]
        lse = rows_ref[0, group, head : head + 1, :width]
        centre = rows_ref[1, group, head : head + 1, :width]
        out = jnp.zeros((HD, width), jnp.float32)
        dquery = jnp.zeros((HD, width), jnp.float32)
        for side in range(2):
            _, _, keys_t, vals_t = sides[group][side]
            scores = pairs[side][0] * (FACTOR * LOG2E) - lse
            if side == 0:
                scores = scores + (bias_ref if head < GROUP else bbias_ref)[...]
            elif head < GROUP:
                scores = scores + tbias_ref[...]
            probs = jnp.exp2(scores)
            dscores = (probs * (pairs[side][1] - centre)).astype(jnp.bfloat16)
            weights = probs.astype(jnp.bfloat16)
            out = out + dot_nn(vals_t, weights)
            dquery = dquery + dot_nn(keys_t, dscores)
            if side == 1:
                key_grad = key_grad + dot_nn(dscores, query)
                val_grad = val_grad + dot_nn(weights, cot)
        out = out.T.astype(jnp.bfloat16)
        dquery = (dquery * FACTOR).T.astype(jnp.bfloat16)
        if head < GROUP:
            at = (group * GROUP + head) * HD
            out_ref[:, at : at + HD] = out
            dq_ref[:, at : at + HD] = dquery
            continue
        for each in range(GROUP):
            at = (group * GROUP + each) * HD
            bout_ref[:, at : at + HD] = out[each * count : (each + 1) * count]
            bdq_ref[:, at : at + HD] = dquery[each * count : (each + 1) * count]
        dkv_ref[:, group * HD : (group + 1) * HD] = (key_grad * FACTOR).astype(jnp.bfloat16)
        dkv_ref[:, (KVH + group) * HD : (KVH + group + 1) * HD] = val_grad.astype(jnp.bfloat16)


VM = pl.BlockSpec(memory_space=pltpu.VMEM)
SM = pl.BlockSpec(memory_space=pltpu.SMEM)


def call(kernel, outs, scratch, specs, args, flops):
    return pl.pallas_call(
        kernel,
        out_shape=outs,
        in_specs=specs,
        out_specs=tuple(VM for _ in outs),
        scratch_shapes=scratch,
        compiler_params=pltpu.CompilerParams(vmem_limit_bytes=16 * 1024 * 1024),
        cost_estimate=pl.CostEstimate(
            flops=flops, bytes_accessed=4 * 1024 * 1024, transcendentals=0
        ),
    )(*args)


def token_stats(query, beacon_query, kv, cot, beacon_cot):
    span = query.shape[0]
    return call(
        token_stats_kernel,
        (jax.ShapeDtypeStruct((3, KVH, GROUP + 1, span), jnp.float32),),
        [pltpu.VMEM((span, span), jnp.float32)],
        [VM] * 5,
        (query, beacon_query, kv, cot, beacon_cot),
        4 * span * span * HD * KVH * (GROUP + 1),
    )[0]


def beacon_grads(pos, query, beacon_query, all_kv, cot, beacon_cot, stats):
    span = query.shape[0]
    total = all_kv.shape[0]
    return call(
        beacon_grad_kernel,
        (
            jax.ShapeDtypeStruct(all_kv.shape, jnp.bfloat16),
            jax.ShapeDtypeStruct((2, KVH, GROUP + 1, span), jnp.float32),
        ),
        [pltpu.VMEM((total, span), jnp.float32), pltpu.VMEM((total, HD), jnp.float32)],
        [SM] + [VM] * 6,
        (pos, query, beacon_query, all_kv, cot, beacon_cot, stats),
        8 * span * total * HD * KVH * (GROUP + 1),
    )


def rest(pos, query, beacon_query, all_kv, kv, cot, beacon_cot, rows):
    span = query.shape[0]
    total = all_kv.shape[0]
    like = lambda x: jax.ShapeDtypeStruct(x.shape, jnp.bfloat16)
    return call(
        rest_kernel,
        (like(query), like(beacon_query), like(query), like(beacon_query), like(kv)),
        [
            pltpu.VMEM((total, span), jnp.float32),
            pltpu.VMEM((total, HD), jnp.float32),
            pltpu.VMEM((span, span), jnp.float32),
        ],
        [SM] + [VM] * 7,
        (pos, query, beacon_query, all_kv, kv, cot, beacon_cot, rows),
        10 * span * (total + span) * HD * KVH * (GROUP + 1),
    )


def partial_kernel(pos_ref, hidden_ref, w0_ref, w1_ref, w2_ref, w3_ref, part_ref, *block_refs):
    line = lax.div(pos_ref[0], jnp.int32(hidden_ref.shape[0]))
    rows = hidden_ref.shape[0] * hidden_ref.shape[2]
    total = jnp.zeros((rows, w0_ref.shape[1]), jnp.float32)
    for step, w_ref in enumerate((w0_ref, w1_ref, w2_ref, w3_ref)):
        block = hidden_ref[:, line ^ step].reshape(rows, w_ref.shape[0])
        block_refs[step][...] = block
        total = total + dot_nn(block, w_ref[...])
    part_ref[...] = total.astype(jnp.bfloat16).reshape(part_ref.shape)


def partial_kv(pos, hidden, weights):
    size, _, rows, depth = hidden.shape
    block = jax.ShapeDtypeStruct((size * rows, depth), jnp.bfloat16)
    part = jax.ShapeDtypeStruct((size, rows, weights[0].shape[1]), jnp.bfloat16)
    return call(
        partial_kernel,
        (part,) + (block,) * LINES,
        [],
        [SM] + [VM] * (1 + LINES),
        (pos, hidden) + tuple(weights),
        2 * LINES * size * rows * depth * weights[0].shape[1],
    )


def hidden_grad_kernel(pos_ref, grad_ref, w0_ref, w1_ref, w2_ref, w3_ref, out_ref):
    line = lax.div(pos_ref[0], jnp.int32(out_ref.shape[0]))
    rows = grad_ref.shape[0] // LINES
    grad = grad_ref[pl.ds(pl.multiple_of(line * rows, rows), rows), :]
    for step, w_ref in enumerate((w0_ref, w1_ref, w2_ref, w3_ref)):
        part = dot_nt(grad, w_ref[...]).astype(jnp.bfloat16)
        out_ref[:, line ^ step] = part.reshape(out_ref.shape[0], out_ref.shape[2], -1)


def hidden_grad_part(pos, all_grad, weights, size):
    total, width = all_grad.shape
    depth = weights[0].shape[0]
    return call(
        hidden_grad_kernel,
        (jax.ShapeDtypeStruct((size, LINES, total // (LINES * size), depth), jnp.bfloat16),),
        [],
        [SM] + [VM] * (1 + LINES),
        (pos, all_grad) + tuple(weights),
        2 * total * width * depth,
    )[0]


def weight_grad_kernel(size, pos_ref, grad_ref, h0_ref, h1_ref, h2_ref, h3_ref, out_ref):
    line = lax.div(pos_ref[0], jnp.int32(size))
    rows = grad_ref.shape[0] // LINES
    total = jnp.zeros(out_ref.shape, jnp.float32)
    for step, h_ref in enumerate((h0_ref, h1_ref, h2_ref, h3_ref)):
        at = pl.multiple_of((line ^ step) * rows, rows)
        total = total + lax.dot_general(
            h_ref[...],
            grad_ref[pl.ds(at, rows), :],
            (((0,), (0,)), ((), ())),
            preferred_element_type=jnp.float32,
        )
    out_ref[...] = total.astype(jnp.bfloat16)


def weight_grad_part(pos, all_grad, hiddens, size):
    return call(
        functools.partial(weight_grad_kernel, size),
        (jax.ShapeDtypeStruct((hiddens[0].shape[1], all_grad.shape[1]), jnp.bfloat16),),
        [],
        [SM] + [VM] * (1 + LINES),
        (pos, all_grad) + tuple(hiddens),
        10**9,
    )[0]


def exchange(blocks):
    return lax.all_to_all(blocks, "ctx", 0, 0, tiled=True)


def exchange_line(blocks):
    size = blocks.shape[0]
    groups = [[line * size + i for i in range(size)] for line in range(LINES)]
    return lax.all_to_all(blocks, "ctx", 0, 0, axis_index_groups=groups, tiled=True)


def swap(rows, axis, mask):
    pairs = [(i, i ^ mask) for i in range(lax.axis_size(axis))]
    return lax.ppermute(rows, axis, pairs)


def sum_dp(sent, beside):
    near, far, wide = [swap(sent, "dp", mask).astype(jnp.float32) for mask in (2, 5, 7)]
    sent, beside = lax.optimization_barrier((sent, beside))
    sent = ((sent.astype(jnp.float32) + near) + (far + wide)).astype(jnp.bfloat16)
    return sent.astype(jnp.float32) + swap(sent, "dp", 1).astype(jnp.float32), beside


def shards(
    query, keys_values, beacon_query, beacon_hidden, beacon_weight, grad_tokens, grad_beacons
):
    count = lax.axis_size("ctx")
    size = count // LINES
    pos = lax.axis_index("ctx").astype(jnp.int32).reshape(1)
    rows = beacon_hidden.shape[1]
    stats = token_stats(
        query[0], beacon_query[0], keys_values[0], grad_tokens[0], grad_beacons[0]
    )

    hidden = beacon_hidden[0].reshape(rows, LINES, size, -1).transpose(2, 1, 0, 3)
    hidden, late_weight = lax.optimization_barrier((hidden, beacon_weight))
    hidden = exchange_line(hidden)
    weights = [beacon_weight] + [
        swap(late_weight, "ctx", step * size) for step in range(1, LINES)
    ]
    part_kv, *blocks = partial_kv(pos, hidden, weights)
    part_kv, stats = lax.optimization_barrier((part_kv, stats))
    own_kv = jnp.sum(exchange_line(part_kv).astype(jnp.float32), 0).astype(jnp.bfloat16)
    all_kv = exchange(jnp.broadcast_to(own_kv[None], (count,) + own_kv.shape))
    all_kv = all_kv.reshape(rows * count, -1)
    columns = [blocks[0]] + [
        swap(blocks[step], "ctx", step * size) for step in range(1, LINES)
    ]
    all_kv, columns = lax.optimization_barrier((all_kv, columns))

    contrib, row_stats = beacon_grads(
        pos, query[0], beacon_query[0], all_kv, grad_tokens[0], grad_beacons[0], stats
    )
    others = rest(
        pos, query[0], beacon_query[0], all_kv, keys_values[0], grad_tokens[0], grad_beacons[0], row_stats
    )
    arrived = exchange(contrib.reshape(count, rows, -1))
    arrived, others = lax.optimization_barrier((arrived, others))
    tokens_out, beacons_out, query_grad, beacon_qgrad, token_kvgrad = others
    own_grad = jnp.sum(arrived.astype(jnp.float32), 0).astype(jnp.bfloat16)
    own_grad = lax.optimization_barrier(own_grad)
    all_grad = exchange(jnp.broadcast_to(own_grad[None], (count,) + own_grad.shape))
    all_grad = all_grad.reshape(rows * count, -1)

    hidden_part = hidden_grad_part(pos, all_grad, weights, size)
    hidden_part, late_grad = lax.optimization_barrier((hidden_part, all_grad))
    weight_part = weight_grad_part(pos, late_grad, columns, size)
    hidden_blocks = exchange_line(hidden_part)
    grad_weight, hidden_blocks = sum_dp(weight_part, hidden_blocks)
    hidden_grad = hidden_blocks.transpose(2, 1, 0, 3).reshape(rows, -1)
    return (
        tokens_out[None],
        beacons_out[None],
        query_grad[None],
        token_kvgrad[None],
        beacon_qgrad[None],
        hidden_grad[None],
        grad_weight,
    )


def solution(mesh):
    placed = (
        P("dp", "ctx", None),
        P("dp", "ctx", None),
        P("dp", "ctx", None),
        P("dp", "ctx", None),
        P("ctx", None),
        P("dp", "ctx", None),
        P("dp", "ctx", None),
    )
    return jax.shard_map(
        shards,
        mesh=mesh,
        in_specs=placed,
        out_specs=(
            P("dp", "ctx", None),
            P("dp", "ctx", None),
            P("dp", "ctx", None),
            P("dp", "ctx", None),
            P("dp", "ctx", None),
            P("dp", "ctx", None),
            P("ctx", None),
        ),
        check_vma=False,
    )
```

```python
import functools

import jax
import jax.numpy as jnp
from jax import lax
from jax.experimental import pallas as pl
from jax.experimental.pallas import tpu as pltpu
from jax.sharding import PartitionSpec as P

KVH = 2
HD = 128
GROUP = 7
LINES = 4
MASKED = -1e30
LOG2E = 1.4426950408889634
FACTOR = HD ** (-0.5)


def dot_nt(left, right):
    return lax.dot_general(
        left, right, (((1,), (1,)), ((), ())), preferred_element_type=jnp.float32
    )


def dot_nn(left, right):
    return jnp.dot(left, right, preferred_element_type=jnp.float32)


def head_rows(tokens_ref, beacons_ref, group, head):
    if head < GROUP:
        start = (group * GROUP + head) * HD
        return tokens_ref[:, start : start + HD]
    parts = []
    for each in range(GROUP):
        start = (group * GROUP + each) * HD
        parts.append(beacons_ref[:, start : start + HD])
    rows = beacons_ref.shape[0]
    parts.append(jnp.zeros((HD - GROUP * rows, HD), beacons_ref.dtype))
    return jnp.concatenate(parts, 0)


def token_bias(span):
    col = lax.broadcasted_iota(jnp.int32, (span, span), 0)
    row = lax.broadcasted_iota(jnp.int32, (span, span), 1)
    return jnp.where(col <= row, 0.0, MASKED).astype(jnp.float32)


def prefix_bias(total, width, start, rank_rows):
    col = lax.broadcasted_iota(jnp.int32, (total, width), 0)
    limit = start
    if rank_rows is not None:
        lane = lax.broadcasted_iota(jnp.int32, (total, width), 1)
        limit = start + 1 + (lane & (rank_rows - 1))
    return jnp.where(col < limit, 0.0, MASKED).astype(jnp.float32)


def token_stats_kernel(q_ref, bq_ref, kv_ref, c_ref, bc_ref, stats_ref, bias_ref):
    span = q_ref.shape[0]
    bias_ref[...] = token_bias(span)
    for group in range(KVH):
        keys = kv_ref[:, group * HD : (group + 1) * HD]
        vals = kv_ref[:, (KVH + group) * HD : (KVH + group + 1) * HD]
        for head in range(GROUP + 1):
            query = head_rows(q_ref, bq_ref, group, head)
            cot = head_rows(c_ref, bc_ref, group, head)
            width = query.shape[0]
            scores = dot_nt(keys, query) * (FACTOR * LOG2E)
            if head < GROUP:
                scores = scores + bias_ref[...]
            top = jnp.max(scores, 0, keepdims=True)
            expo = jnp.exp2(scores - top)
            dweights = dot_nt(vals, cot)
            stats_ref[0, group, head : head + 1, :width] = top
            stats_ref[1, group, head : head + 1, :width] = jnp.sum(expo, 0, keepdims=True)
            stats_ref[2, group, head : head + 1, :width] = jnp.sum(
                expo * dweights, 0, keepdims=True
            )


def beacon_grad_kernel(
    pos_ref, q_ref, bq_ref, kv_ref, c_ref, bc_ref, stats_ref, contrib_ref, rows_ref, bias_ref, bbias_ref
):
    total = kv_ref.shape[0]
    span = q_ref.shape[0]
    count = bq_ref.shape[0]
    start = pos_ref[0] * count
    bias_ref[...] = prefix_bias(total, span, start, None)
    bbias_ref[...] = prefix_bias(total, HD, start, count)
    jobs = [(group, head) for group in range(KVH) for head in range(GROUP + 1)]

    def products(group, head):
        query = head_rows(q_ref, bq_ref, group, head)
        cot = head_rows(c_ref, bc_ref, group, head)
        keys = kv_ref[:, group * HD : (group + 1) * HD]
        vals = kv_ref[:, (KVH + group) * HD : (KVH + group + 1) * HD]
        return query, cot, dot_nt(keys, query), dot_nt(vals, cot)

    ahead = products(*jobs[0])
    for at, (group, head) in enumerate(jobs):
        query, cot, scores, dweights = ahead
        if at + 1 < len(jobs):
            ahead = products(*jobs[at + 1])
        if head == 0:
            key_grad = jnp.zeros((total, HD), jnp.float32)
            val_grad = jnp.zeros((total, HD), jnp.float32)
        width = query.shape[0]
        bias = bias_ref if head < GROUP else bbias_ref
        scores = scores * (FACTOR * LOG2E) + bias[...]
        top_tok = stats_ref[0, group, head : head + 1, :width]
        sum_tok = stats_ref[1, group, head : head + 1, :width]
        cen_tok = stats_ref[2, group, head : head + 1, :width]
        top = jnp.maximum(jnp.max(scores, 0, keepdims=True), top_tok)
        shift = jnp.exp2(top_tok - top)
        expo = jnp.exp2(scores - top)
        total_sum = shift * sum_tok + jnp.sum(expo, 0, keepdims=True)
        inverse = 1.0 / total_sum
        centre = inverse * (shift * cen_tok + jnp.sum(expo * dweights, 0, keepdims=True))
        probs = expo * inverse
        dscores = (probs * (dweights - centre)).astype(jnp.bfloat16)
        key_grad = key_grad + dot_nn(dscores, query)
        val_grad = val_grad + dot_nn(probs.astype(jnp.bfloat16), cot)
        rows_ref[0, group, head : head + 1, :width] = top + jnp.log(total_sum) * LOG2E
        rows_ref[1, group, head : head + 1, :width] = centre
        if head == GROUP:
            contrib_ref[:, group * HD : (group + 1) * HD] = (key_grad * FACTOR).astype(jnp.bfloat16)
            contrib_ref[:, (KVH + group) * HD : (KVH + group + 1) * HD] = val_grad.astype(
                jnp.bfloat16
            )


def rest_kernel(
    pos_ref, q_ref, bq_ref, bkv_ref, kv_ref, c_ref, bc_ref, rows_ref,
    out_ref, bout_ref, dq_ref, bdq_ref, dkv_ref, bias_ref, bbias_ref, tbias_ref,
):
    total = bkv_ref.shape[0]
    span = q_ref.shape[0]
    count = bq_ref.shape[0]
    start = pos_ref[0] * count
    bias_ref[...] = prefix_bias(total, span, start, None)
    bbias_ref[...] = prefix_bias(total, HD, start, count)
    tbias_ref[...] = token_bias(span)
    jobs = [(group, head) for group in range(KVH) for head in range(GROUP + 1)]
    sides = []
    for group in range(KVH):
        key_cols = slice(group * HD, (group + 1) * HD)
        val_cols = slice((KVH + group) * HD, (KVH + group + 1) * HD)
        both = [(ref[:, key_cols], ref[:, val_cols]) for ref in (bkv_ref, kv_ref)]
        sides.append([(keys, vals, keys.T, vals.T) for keys, vals in both])

    def products(group, head):
        query = head_rows(q_ref, bq_ref, group, head)
        cot = head_rows(c_ref, bc_ref, group, head)
        pairs = [(dot_nt(side[0], query), dot_nt(side[1], cot)) for side in sides[group]]
        return query, cot, pairs

    ahead = products(*jobs[0])
    for job, (group, head) in enumerate(jobs):
        query, cot, pairs = ahead
        if job + 1 < len(jobs):
            ahead = products(*jobs[job + 1])
        if head == 0:
            key_grad = jnp.zeros((span, HD), jnp.float32)
            val_grad = jnp.zeros((span, HD), jnp.float32)
        width = query.shape[0]
        lse = rows_ref[0, group, head : head + 1, :width]
        centre = rows_ref[1, group, head : head + 1, :width]
        out = jnp.zeros((HD, width), jnp.float32)
        dquery = jnp.zeros((HD, width), jnp.float32)
        for side in range(2):
            _, _, keys_t, vals_t = sides[group][side]
            scores = pairs[side][0] * (FACTOR * LOG2E) - lse
            if side == 0:
                scores = scores + (bias_ref if head < GROUP else bbias_ref)[...]
            elif head < GROUP:
                scores = scores + tbias_ref[...]
            probs = jnp.exp2(scores)
            dscores = (probs * (pairs[side][1] - centre)).astype(jnp.bfloat16)
            weights = probs.astype(jnp.bfloat16)
            out = out + dot_nn(vals_t, weights)
            dquery = dquery + dot_nn(keys_t, dscores)
            if side == 1:
                key_grad = key_grad + dot_nn(dscores, query)
                val_grad = val_grad + dot_nn(weights, cot)
        out = out.T.astype(jnp.bfloat16)
        dquery = (dquery * FACTOR).T.astype(jnp.bfloat16)
        if head < GROUP:
            at = (group * GROUP + head) * HD
            out_ref[:, at : at + HD] = out
            dq_ref[:, at : at + HD] = dquery
            continue
        for each in range(GROUP):
            at = (group * GROUP + each) * HD
            bout_ref[:, at : at + HD] = out[each * count : (each + 1) * count]
            bdq_ref[:, at : at + HD] = dquery[each * count : (each + 1) * count]
        dkv_ref[:, group * HD : (group + 1) * HD] = (key_grad * FACTOR).astype(jnp.bfloat16)
        dkv_ref[:, (KVH + group) * HD : (KVH + group + 1) * HD] = val_grad.astype(jnp.bfloat16)


VM = pl.BlockSpec(memory_space=pltpu.VMEM)
SM = pl.BlockSpec(memory_space=pltpu.SMEM)


def call(kernel, outs, scratch, specs, args, flops):
    return pl.pallas_call(
        kernel,
        out_shape=outs,
        in_specs=specs,
        out_specs=tuple(VM for _ in outs),
        scratch_shapes=scratch,
        compiler_params=pltpu.CompilerParams(vmem_limit_bytes=16 * 1024 * 1024),
        cost_estimate=pl.CostEstimate(
            flops=flops, bytes_accessed=4 * 1024 * 1024, transcendentals=0
        ),
    )(*args)


def token_stats(query, beacon_query, kv, cot, beacon_cot):
    span = query.shape[0]
    return call(
        token_stats_kernel,
        (jax.ShapeDtypeStruct((3, KVH, GROUP + 1, span), jnp.float32),),
        [pltpu.VMEM((span, span), jnp.float32)],
        [VM] * 5,
        (query, beacon_query, kv, cot, beacon_cot),
        4 * span * span * HD * KVH * (GROUP + 1),
    )[0]


def beacon_grads(pos, query, beacon_query, all_kv, cot, beacon_cot, stats):
    span = query.shape[0]
    total = all_kv.shape[0]
    return call(
        beacon_grad_kernel,
        (
            jax.ShapeDtypeStruct(all_kv.shape, jnp.bfloat16),
            jax.ShapeDtypeStruct((2, KVH, GROUP + 1, span), jnp.float32),
        ),
        [pltpu.VMEM((total, span), jnp.float32), pltpu.VMEM((total, HD), jnp.float32)],
        [SM] + [VM] * 6,
        (pos, query, beacon_query, all_kv, cot, beacon_cot, stats),
        8 * span * total * HD * KVH * (GROUP + 1),
    )


def rest(pos, query, beacon_query, all_kv, kv, cot, beacon_cot, rows):
    span = query.shape[0]
    total = all_kv.shape[0]
    like = lambda x: jax.ShapeDtypeStruct(x.shape, jnp.bfloat16)
    return call(
        rest_kernel,
        (like(query), like(beacon_query), like(query), like(beacon_query), like(kv)),
        [
            pltpu.VMEM((total, span), jnp.float32),
            pltpu.VMEM((total, HD), jnp.float32),
            pltpu.VMEM((span, span), jnp.float32),
        ],
        [SM] + [VM] * 7,
        (pos, query, beacon_query, all_kv, kv, cot, beacon_cot, rows),
        10 * span * (total + span) * HD * KVH * (GROUP + 1),
    )


def partial_kernel(pos_ref, hidden_ref, w0_ref, w1_ref, w2_ref, w3_ref, part_ref, *block_refs):
    line = lax.div(pos_ref[0], jnp.int32(hidden_ref.shape[0]))
    rows = hidden_ref.shape[0] * hidden_ref.shape[2]
    total = jnp.zeros((rows, w0_ref.shape[1]), jnp.float32)
    for step, w_ref in enumerate((w0_ref, w1_ref, w2_ref, w3_ref)):
        block = hidden_ref[:, line ^ step].reshape(rows, w_ref.shape[0])
        block_refs[step][...] = block
        total = total + dot_nn(block, w_ref[...])
    part_ref[...] = total.astype(jnp.bfloat16).reshape(part_ref.shape)


def partial_kv(pos, hidden, weights):
    size, _, rows, depth = hidden.shape
    block = jax.ShapeDtypeStruct((size * rows, depth), jnp.bfloat16)
    part = jax.ShapeDtypeStruct((size, rows, weights[0].shape[1]), jnp.bfloat16)
    return call(
        partial_kernel,
        (part,) + (block,) * LINES,
        [],
        [SM] + [VM] * (1 + LINES),
        (pos, hidden) + tuple(weights),
        2 * LINES * size * rows * depth * weights[0].shape[1],
    )


def hidden_grad_kernel(pos_ref, grad_ref, w0_ref, w1_ref, w2_ref, w3_ref, out_ref):
    line = lax.div(pos_ref[0], jnp.int32(out_ref.shape[0]))
    rows = grad_ref.shape[0] // LINES
    grad = grad_ref[pl.ds(pl.multiple_of(line * rows, rows), rows), :]
    for step, w_ref in enumerate((w0_ref, w1_ref, w2_ref, w3_ref)):
        part = dot_nt(grad, w_ref[...]).astype(jnp.bfloat16)
        out_ref[:, line ^ step] = part.reshape(out_ref.shape[0], out_ref.shape[2], -1)


def hidden_grad_part(pos, all_grad, weights, size):
    total, width = all_grad.shape
    depth = weights[0].shape[0]
    return call(
        hidden_grad_kernel,
        (jax.ShapeDtypeStruct((size, LINES, total // (LINES * size), depth), jnp.bfloat16),),
        [],
        [SM] + [VM] * (1 + LINES),
        (pos, all_grad) + tuple(weights),
        2 * total * width * depth,
    )[0]


def weight_grad_kernel(size, pos_ref, grad_ref, h0_ref, h1_ref, h2_ref, h3_ref, out_ref):
    line = lax.div(pos_ref[0], jnp.int32(size))
    rows = grad_ref.shape[0] // LINES
    total = jnp.zeros(out_ref.shape, jnp.float32)
    for step, h_ref in enumerate((h0_ref, h1_ref, h2_ref, h3_ref)):
        at = pl.multiple_of((line ^ step) * rows, rows)
        total = total + lax.dot_general(
            h_ref[...],
            grad_ref[pl.ds(at, rows), :],
            (((0,), (0,)), ((), ())),
            preferred_element_type=jnp.float32,
        )
    out_ref[...] = total.astype(jnp.bfloat16)


def weight_grad_part(pos, all_grad, hiddens, size):
    return call(
        functools.partial(weight_grad_kernel, size),
        (jax.ShapeDtypeStruct((hiddens[0].shape[1], all_grad.shape[1]), jnp.bfloat16),),
        [],
        [SM] + [VM] * (1 + LINES),
        (pos, all_grad) + tuple(hiddens),
        10**9,
    )[0]


def exchange(blocks):
    return lax.all_to_all(blocks, "ctx", 0, 0, tiled=True)


def exchange_line(blocks):
    size = blocks.shape[0]
    groups = [[line * size + i for i in range(size)] for line in range(LINES)]
    return lax.all_to_all(blocks, "ctx", 0, 0, axis_index_groups=groups, tiled=True)


def swap(rows, axis, mask):
    pairs = [(i, i ^ mask) for i in range(lax.axis_size(axis))]
    return lax.ppermute(rows, axis, pairs)


def sum_dp(sent, beside):
    near, far, wide = [swap(sent, "dp", mask).astype(jnp.float32) for mask in (3, 5, 6)]
    sent, beside = lax.optimization_barrier((sent, beside))
    sent = ((sent.astype(jnp.float32) + near) + (far + wide)).astype(jnp.bfloat16)
    return sent.astype(jnp.float32) + swap(sent, "dp", 1).astype(jnp.float32), beside


def shards(
    query, keys_values, beacon_query, beacon_hidden, beacon_weight, grad_tokens, grad_beacons
):
    count = lax.axis_size("ctx")
    size = count // LINES
    pos = lax.axis_index("ctx").astype(jnp.int32).reshape(1)
    rows = beacon_hidden.shape[1]
    stats = token_stats(
        query[0], beacon_query[0], keys_values[0], grad_tokens[0], grad_beacons[0]
    )

    hidden = beacon_hidden[0].reshape(rows, LINES, size, -1).transpose(2, 1, 0, 3)
    hidden, late_weight = lax.optimization_barrier((hidden, beacon_weight))
    hidden = exchange_line(hidden)
    weights = [beacon_weight] + [
        swap(late_weight, "ctx", step * size) for step in range(1, LINES)
    ]
    part_kv, *blocks = partial_kv(pos, hidden, weights)
    part_kv, stats = lax.optimization_barrier((part_kv, stats))
    own_kv = jnp.sum(exchange_line(part_kv).astype(jnp.float32), 0).astype(jnp.bfloat16)
    all_kv = exchange(jnp.broadcast_to(own_kv[None], (count,) + own_kv.shape))
    all_kv = all_kv.reshape(rows * count, -1)
    columns = [blocks[0]] + [
        swap(blocks[step], "ctx", step * size) for step in range(1, LINES)
    ]
    all_kv, columns = lax.optimization_barrier((all_kv, columns))

    contrib, row_stats = beacon_grads(
        pos, query[0], beacon_query[0], all_kv, grad_tokens[0], grad_beacons[0], stats
    )
    others = rest(
        pos, query[0], beacon_query[0], all_kv, keys_values[0], grad_tokens[0], grad_beacons[0], row_stats
    )
    arrived = exchange(contrib.reshape(count, rows, -1))
    arrived, others = lax.optimization_barrier((arrived, others))
    tokens_out, beacons_out, query_grad, beacon_qgrad, token_kvgrad = others
    own_grad = jnp.sum(arrived.astype(jnp.float32), 0).astype(jnp.bfloat16)
    own_grad = lax.optimization_barrier(own_grad)
    all_grad = exchange(jnp.broadcast_to(own_grad[None], (count,) + own_grad.shape))
    all_grad = all_grad.reshape(rows * count, -1)

    hidden_part = hidden_grad_part(pos, all_grad, weights, size)
    hidden_part, late_grad = lax.optimization_barrier((hidden_part, all_grad))
    weight_part = weight_grad_part(pos, late_grad, columns, size)
    hidden_blocks = exchange_line(hidden_part)
    grad_weight, hidden_blocks = sum_dp(weight_part, hidden_blocks)
    hidden_grad = hidden_blocks.transpose(2, 1, 0, 3).reshape(rows, -1)
    return (
        tokens_out[None],
        beacons_out[None],
        query_grad[None],
        token_kvgrad[None],
        beacon_qgrad[None],
        hidden_grad[None],
        grad_weight,
    )


def solution(mesh):
    placed = (
        P("dp", "ctx", None),
        P("dp", "ctx", None),
        P("dp", "ctx", None),
        P("dp", "ctx", None),
        P("ctx", None),
        P("dp", "ctx", None),
        P("dp", "ctx", None),
    )
    return jax.shard_map(
        shards,
        mesh=mesh,
        in_specs=placed,
        out_specs=(
            P("dp", "ctx", None),
            P("dp", "ctx", None),
            P("dp", "ctx", None),
            P("dp", "ctx", None),
            P("dp", "ctx", None),
            P("dp", "ctx", None),
            P("ctx", None),
        ),
        check_vma=False,
    )
```

```python
import functools

import jax
import jax.numpy as jnp
from jax import lax
from jax.experimental import pallas as pl
from jax.experimental.pallas import tpu as pltpu
from jax.sharding import PartitionSpec as P

KVH = 2
HD = 128
GROUP = 7
LINES = 4
MASKED = -1e30
LOG2E = 1.4426950408889634
FACTOR = HD ** (-0.5)


def dot_nt(left, right):
    return lax.dot_general(
        left, right, (((1,), (1,)), ((), ())), preferred_element_type=jnp.float32
    )


def dot_nn(left, right):
    return jnp.dot(left, right, preferred_element_type=jnp.float32)


def head_rows(tokens_ref, beacons_ref, group, head):
    if head < GROUP:
        start = (group * GROUP + head) * HD
        return tokens_ref[:, start : start + HD]
    parts = []
    for each in range(GROUP):
        start = (group * GROUP + each) * HD
        parts.append(beacons_ref[:, start : start + HD])
    rows = beacons_ref.shape[0]
    parts.append(jnp.zeros((HD - GROUP * rows, HD), beacons_ref.dtype))
    return jnp.concatenate(parts, 0)


def token_bias(span):
    col = lax.broadcasted_iota(jnp.int32, (span, span), 0)
    row = lax.broadcasted_iota(jnp.int32, (span, span), 1)
    return jnp.where(col <= row, 0.0, MASKED).astype(jnp.float32)


def prefix_bias(total, width, start, rank_rows):
    col = lax.broadcasted_iota(jnp.int32, (total, width), 0)
    limit = start
    if rank_rows is not None:
        lane = lax.broadcasted_iota(jnp.int32, (total, width), 1)
        limit = start + 1 + (lane & (rank_rows - 1))
    return jnp.where(col < limit, 0.0, MASKED).astype(jnp.float32)


def token_stats_kernel(q_ref, bq_ref, kv_ref, c_ref, bc_ref, stats_ref, bias_ref):
    span = q_ref.shape[0]
    bias_ref[...] = token_bias(span)
    for group in range(KVH):
        keys = kv_ref[:, group * HD : (group + 1) * HD]
        vals = kv_ref[:, (KVH + group) * HD : (KVH + group + 1) * HD]
        for head in range(GROUP + 1):
            query = head_rows(q_ref, bq_ref, group, head)
            cot = head_rows(c_ref, bc_ref, group, head)
            width = query.shape[0]
            scores = dot_nt(keys, query) * (FACTOR * LOG2E)
            if head < GROUP:
                scores = scores + bias_ref[...]
            top = jnp.max(scores, 0, keepdims=True)
            expo = jnp.exp2(scores - top)
            dweights = dot_nt(vals, cot)
            stats_ref[0, group, head : head + 1, :width] = top
            stats_ref[1, group, head : head + 1, :width] = jnp.sum(expo, 0, keepdims=True)
            stats_ref[2, group, head : head + 1, :width] = jnp.sum(
                expo * dweights, 0, keepdims=True
            )


def beacon_grad_kernel(
    pos_ref, q_ref, bq_ref, kv_ref, c_ref, bc_ref, stats_ref, contrib_ref, rows_ref, bias_ref, bbias_ref
):
    total = kv_ref.shape[0]
    span = q_ref.shape[0]
    count = bq_ref.shape[0]
    start = pos_ref[0] * count
    bias_ref[...] = prefix_bias(total, span, start, None)
    bbias_ref[...] = prefix_bias(total, HD, start, count)
    jobs = [(group, head) for group in range(KVH) for head in range(GROUP + 1)]

    def products(group, head):
        query = head_rows(q_ref, bq_ref, group, head)
        cot = head_rows(c_ref, bc_ref, group, head)
        keys = kv_ref[:, group * HD : (group + 1) * HD]
        vals = kv_ref[:, (KVH + group) * HD : (KVH + group + 1) * HD]
        return query, cot, dot_nt(keys, query), dot_nt(vals, cot)

    ahead = products(*jobs[0])
    for at, (group, head) in enumerate(jobs):
        query, cot, scores, dweights = ahead
        if at + 1 < len(jobs):
            ahead = products(*jobs[at + 1])
        if head == 0:
            key_grad = jnp.zeros((total, HD), jnp.float32)
            val_grad = jnp.zeros((total, HD), jnp.float32)
        width = query.shape[0]
        bias = bias_ref if head < GROUP else bbias_ref
        scores = scores * (FACTOR * LOG2E) + bias[...]
        top_tok = stats_ref[0, group, head : head + 1, :width]
        sum_tok = stats_ref[1, group, head : head + 1, :width]
        cen_tok = stats_ref[2, group, head : head + 1, :width]
        top = jnp.maximum(jnp.max(scores, 0, keepdims=True), top_tok)
        shift = jnp.exp2(top_tok - top)
        expo = jnp.exp2(scores - top)
        total_sum = shift * sum_tok + jnp.sum(expo, 0, keepdims=True)
        inverse = 1.0 / total_sum
        centre = inverse * (shift * cen_tok + jnp.sum(expo * dweights, 0, keepdims=True))
        weights = (expo * inverse).astype(jnp.bfloat16)
        dscores = weights * (dweights - centre).astype(jnp.bfloat16)
        key_grad = key_grad + dot_nn(dscores, query)
        val_grad = val_grad + dot_nn(weights, cot)
        rows_ref[0, group, head : head + 1, :width] = top + jnp.log(total_sum) * LOG2E
        rows_ref[1, group, head : head + 1, :width] = centre
        if head == GROUP:
            contrib_ref[:, group * HD : (group + 1) * HD] = (key_grad * FACTOR).astype(jnp.bfloat16)
            contrib_ref[:, (KVH + group) * HD : (KVH + group + 1) * HD] = val_grad.astype(
                jnp.bfloat16
            )


def rest_kernel(
    pos_ref, q_ref, bq_ref, bkv_ref, kv_ref, c_ref, bc_ref, rows_ref,
    out_ref, bout_ref, dq_ref, bdq_ref, dkv_ref, bias_ref, bbias_ref, tbias_ref,
):
    total = bkv_ref.shape[0]
    span = q_ref.shape[0]
    count = bq_ref.shape[0]
    start = pos_ref[0] * count
    bias_ref[...] = prefix_bias(total, span, start, None)
    bbias_ref[...] = prefix_bias(total, HD, start, count)
    tbias_ref[...] = token_bias(span)
    jobs = [(group, head) for group in range(KVH) for head in range(GROUP + 1)]
    sides = []
    for group in range(KVH):
        key_cols = slice(group * HD, (group + 1) * HD)
        val_cols = slice((KVH + group) * HD, (KVH + group + 1) * HD)
        both = [(ref[:, key_cols], ref[:, val_cols]) for ref in (bkv_ref, kv_ref)]
        sides.append([(keys, vals, keys.T, vals.T) for keys, vals in both])

    def products(group, head):
        query = head_rows(q_ref, bq_ref, group, head)
        cot = head_rows(c_ref, bc_ref, group, head)
        pairs = [(dot_nt(side[0], query), dot_nt(side[1], cot)) for side in sides[group]]
        return query, cot, pairs

    ahead = products(*jobs[0])
    for job, (group, head) in enumerate(jobs):
        query, cot, pairs = ahead
        if job + 1 < len(jobs):
            ahead = products(*jobs[job + 1])
        if head == 0:
            key_grad = jnp.zeros((span, HD), jnp.float32)
            val_grad = jnp.zeros((span, HD), jnp.float32)
        width = query.shape[0]
        lse = rows_ref[0, group, head : head + 1, :width]
        centre = rows_ref[1, group, head : head + 1, :width]
        out = jnp.zeros((HD, width), jnp.float32)
        dquery = jnp.zeros((HD, width), jnp.float32)
        for side in range(2):
            _, _, keys_t, vals_t = sides[group][side]
            scores = pairs[side][0] * (FACTOR * LOG2E) - lse
            if side == 0:
                scores = scores + (bias_ref if head < GROUP else bbias_ref)[...]
            elif head < GROUP:
                scores = scores + tbias_ref[...]
            weights = jnp.exp2(scores).astype(jnp.bfloat16)
            dscores = weights * (pairs[side][1] - centre).astype(jnp.bfloat16)
            out = out + dot_nn(vals_t, weights)
            dquery = dquery + dot_nn(keys_t, dscores)
            if side == 1:
                key_grad = key_grad + dot_nn(dscores, query)
                val_grad = val_grad + dot_nn(weights, cot)
        out = out.T.astype(jnp.bfloat16)
        dquery = (dquery * FACTOR).T.astype(jnp.bfloat16)
        if head < GROUP:
            at = (group * GROUP + head) * HD
            out_ref[:, at : at + HD] = out
            dq_ref[:, at : at + HD] = dquery
            continue
        for each in range(GROUP):
            at = (group * GROUP + each) * HD
            bout_ref[:, at : at + HD] = out[each * count : (each + 1) * count]
            bdq_ref[:, at : at + HD] = dquery[each * count : (each + 1) * count]
        dkv_ref[:, group * HD : (group + 1) * HD] = (key_grad * FACTOR).astype(jnp.bfloat16)
        dkv_ref[:, (KVH + group) * HD : (KVH + group + 1) * HD] = val_grad.astype(jnp.bfloat16)


VM = pl.BlockSpec(memory_space=pltpu.VMEM)
SM = pl.BlockSpec(memory_space=pltpu.SMEM)


def call(kernel, outs, scratch, specs, args, flops):
    return pl.pallas_call(
        kernel,
        out_shape=outs,
        in_specs=specs,
        out_specs=tuple(VM for _ in outs),
        scratch_shapes=scratch,
        compiler_params=pltpu.CompilerParams(vmem_limit_bytes=16 * 1024 * 1024),
        cost_estimate=pl.CostEstimate(
            flops=flops, bytes_accessed=4 * 1024 * 1024, transcendentals=0
        ),
    )(*args)


def token_stats(query, beacon_query, kv, cot, beacon_cot):
    span = query.shape[0]
    return call(
        token_stats_kernel,
        (jax.ShapeDtypeStruct((3, KVH, GROUP + 1, span), jnp.float32),),
        [pltpu.VMEM((span, span), jnp.float32)],
        [VM] * 5,
        (query, beacon_query, kv, cot, beacon_cot),
        4 * span * span * HD * KVH * (GROUP + 1),
    )[0]


def beacon_grads(pos, query, beacon_query, all_kv, cot, beacon_cot, stats):
    span = query.shape[0]
    total = all_kv.shape[0]
    return call(
        beacon_grad_kernel,
        (
            jax.ShapeDtypeStruct(all_kv.shape, jnp.bfloat16),
            jax.ShapeDtypeStruct((2, KVH, GROUP + 1, span), jnp.float32),
        ),
        [pltpu.VMEM((total, span), jnp.float32), pltpu.VMEM((total, HD), jnp.float32)],
        [SM] + [VM] * 6,
        (pos, query, beacon_query, all_kv, cot, beacon_cot, stats),
        8 * span * total * HD * KVH * (GROUP + 1),
    )


def rest(pos, query, beacon_query, all_kv, kv, cot, beacon_cot, rows):
    span = query.shape[0]
    total = all_kv.shape[0]
    like = lambda x: jax.ShapeDtypeStruct(x.shape, jnp.bfloat16)
    return call(
        rest_kernel,
        (like(query), like(beacon_query), like(query), like(beacon_query), like(kv)),
        [
            pltpu.VMEM((total, span), jnp.float32),
            pltpu.VMEM((total, HD), jnp.float32),
            pltpu.VMEM((span, span), jnp.float32),
        ],
        [SM] + [VM] * 7,
        (pos, query, beacon_query, all_kv, kv, cot, beacon_cot, rows),
        10 * span * (total + span) * HD * KVH * (GROUP + 1),
    )


def partial_kernel(pos_ref, hidden_ref, w0_ref, w1_ref, w2_ref, w3_ref, part_ref, *block_refs):
    line = lax.div(pos_ref[0], jnp.int32(hidden_ref.shape[0]))
    rows = hidden_ref.shape[0] * hidden_ref.shape[2]
    total = jnp.zeros((rows, w0_ref.shape[1]), jnp.float32)
    for step, w_ref in enumerate((w0_ref, w1_ref, w2_ref, w3_ref)):
        block = hidden_ref[:, line ^ step].reshape(rows, w_ref.shape[0])
        block_refs[step][...] = block
        total = total + dot_nn(block, w_ref[...])
    part_ref[...] = total.astype(jnp.bfloat16).reshape(part_ref.shape)


def partial_kv(pos, hidden, weights):
    size, _, rows, depth = hidden.shape
    block = jax.ShapeDtypeStruct((size * rows, depth), jnp.bfloat16)
    part = jax.ShapeDtypeStruct((size, rows, weights[0].shape[1]), jnp.bfloat16)
    return call(
        partial_kernel,
        (part,) + (block,) * LINES,
        [],
        [SM] + [VM] * (1 + LINES),
        (pos, hidden) + tuple(weights),
        2 * LINES * size * rows * depth * weights[0].shape[1],
    )


def hidden_grad_kernel(pos_ref, grad_ref, w0_ref, w1_ref, w2_ref, w3_ref, out_ref):
    line = lax.div(pos_ref[0], jnp.int32(out_ref.shape[0]))
    rows = grad_ref.shape[0] // LINES
    grad = grad_ref[pl.ds(pl.multiple_of(line * rows, rows), rows), :]
    for step, w_ref in enumerate((w0_ref, w1_ref, w2_ref, w3_ref)):
        part = dot_nt(grad, w_ref[...]).astype(jnp.bfloat16)
        out_ref[:, line ^ step] = part.reshape(out_ref.shape[0], out_ref.shape[2], -1)


def hidden_grad_part(pos, all_grad, weights, size):
    total, width = all_grad.shape
    depth = weights[0].shape[0]
    return call(
        hidden_grad_kernel,
        (jax.ShapeDtypeStruct((size, LINES, total // (LINES * size), depth), jnp.bfloat16),),
        [],
        [SM] + [VM] * (1 + LINES),
        (pos, all_grad) + tuple(weights),
        2 * total * width * depth,
    )[0]


def weight_grad_kernel(size, pos_ref, grad_ref, h0_ref, h1_ref, h2_ref, h3_ref, out_ref):
    line = lax.div(pos_ref[0], jnp.int32(size))
    rows = grad_ref.shape[0] // LINES
    total = jnp.zeros(out_ref.shape, jnp.float32)
    for step, h_ref in enumerate((h0_ref, h1_ref, h2_ref, h3_ref)):
        at = pl.multiple_of((line ^ step) * rows, rows)
        total = total + lax.dot_general(
            h_ref[...],
            grad_ref[pl.ds(at, rows), :],
            (((0,), (0,)), ((), ())),
            preferred_element_type=jnp.float32,
        )
    out_ref[...] = total.astype(jnp.bfloat16)


def weight_grad_part(pos, all_grad, hiddens, size):
    return call(
        functools.partial(weight_grad_kernel, size),
        (jax.ShapeDtypeStruct((hiddens[0].shape[1], all_grad.shape[1]), jnp.bfloat16),),
        [],
        [SM] + [VM] * (1 + LINES),
        (pos, all_grad) + tuple(hiddens),
        10**9,
    )[0]


def exchange(blocks):
    return lax.all_to_all(blocks, "ctx", 0, 0, tiled=True)


def exchange_line(blocks):
    size = blocks.shape[0]
    groups = [[line * size + i for i in range(size)] for line in range(LINES)]
    return lax.all_to_all(blocks, "ctx", 0, 0, axis_index_groups=groups, tiled=True)


def swap(rows, axis, mask):
    pairs = [(i, i ^ mask) for i in range(lax.axis_size(axis))]
    return lax.ppermute(rows, axis, pairs)


def sum_dp(sent, beside):
    near, far, wide = [swap(sent, "dp", mask).astype(jnp.float32) for mask in (3, 5, 6)]
    sent, beside = lax.optimization_barrier((sent, beside))
    sent = ((sent.astype(jnp.float32) + near) + (far + wide)).astype(jnp.bfloat16)
    return sent.astype(jnp.float32) + swap(sent, "dp", 1).astype(jnp.float32), beside


def shards(
    query, keys_values, beacon_query, beacon_hidden, beacon_weight, grad_tokens, grad_beacons
):
    count = lax.axis_size("ctx")
    size = count // LINES
    pos = lax.axis_index("ctx").astype(jnp.int32).reshape(1)
    rows = beacon_hidden.shape[1]
    stats = token_stats(
        query[0], beacon_query[0], keys_values[0], grad_tokens[0], grad_beacons[0]
    )

    hidden = beacon_hidden[0].reshape(rows, LINES, size, -1).transpose(2, 1, 0, 3)
    hidden, late_weight = lax.optimization_barrier((hidden, beacon_weight))
    hidden = exchange_line(hidden)
    weights = [beacon_weight] + [
        swap(late_weight, "ctx", step * size) for step in range(1, LINES)
    ]
    part_kv, *blocks = partial_kv(pos, hidden, weights)
    part_kv, stats = lax.optimization_barrier((part_kv, stats))
    own_kv = jnp.sum(exchange_line(part_kv).astype(jnp.float32), 0).astype(jnp.bfloat16)
    all_kv = exchange(jnp.broadcast_to(own_kv[None], (count,) + own_kv.shape))
    all_kv = all_kv.reshape(rows * count, -1)
    columns = [blocks[0]] + [
        swap(blocks[step], "ctx", step * size) for step in range(1, LINES)
    ]
    all_kv, columns = lax.optimization_barrier((all_kv, columns))

    contrib, row_stats = beacon_grads(
        pos, query[0], beacon_query[0], all_kv, grad_tokens[0], grad_beacons[0], stats
    )
    others = rest(
        pos, query[0], beacon_query[0], all_kv, keys_values[0], grad_tokens[0], grad_beacons[0], row_stats
    )
    arrived = exchange(contrib.reshape(count, rows, -1))
    arrived, others = lax.optimization_barrier((arrived, others))
    tokens_out, beacons_out, query_grad, beacon_qgrad, token_kvgrad = others
    own_grad = jnp.sum(arrived.astype(jnp.float32), 0).astype(jnp.bfloat16)
    own_grad = lax.optimization_barrier(own_grad)
    all_grad = exchange(jnp.broadcast_to(own_grad[None], (count,) + own_grad.shape))
    all_grad = all_grad.reshape(rows * count, -1)

    hidden_part = hidden_grad_part(pos, all_grad, weights, size)
    hidden_part, late_grad = lax.optimization_barrier((hidden_part, all_grad))
    weight_part = weight_grad_part(pos, late_grad, columns, size)
    hidden_blocks = exchange_line(hidden_part)
    grad_weight, hidden_blocks = sum_dp(weight_part, hidden_blocks)
    hidden_grad = hidden_blocks.transpose(2, 1, 0, 3).reshape(rows, -1)
    return (
        tokens_out[None],
        beacons_out[None],
        query_grad[None],
        token_kvgrad[None],
        beacon_qgrad[None],
        hidden_grad[None],
        grad_weight,
    )


def solution(mesh):
    placed = (
        P("dp", "ctx", None),
        P("dp", "ctx", None),
        P("dp", "ctx", None),
        P("dp", "ctx", None),
        P("ctx", None),
        P("dp", "ctx", None),
        P("dp", "ctx", None),
    )
    return jax.shard_map(
        shards,
        mesh=mesh,
        in_specs=placed,
        out_specs=(
            P("dp", "ctx", None),
            P("dp", "ctx", None),
            P("dp", "ctx", None),
            P("dp", "ctx", None),
            P("dp", "ctx", None),
            P("dp", "ctx", None),
            P("ctx", None),
        ),
        check_vma=False,
    )
```
